256 devices in a mesh: dp: 32 (over y_lo, z, core), space: 8 (over x, y_hi).
Axes of the slice: x: 4, y: 4 (y_hi: 2, y_lo: 2; y = y_hi * 2 + y_lo), z: 8, core: 2. Of those that a mesh axis runs over, the one named last changes fastest.
Arguments:
- volumes: bfloat16 [32, 32, 32, 8, 128], P('dp', None, 'space'), may hold values from -6 to 6
- w_first: bfloat16 [864, 64], P('dp'), may hold values from -0.21875 to 0.21875
- w_second: bfloat16 [1728, 128], P('dp'), may hold values from -0.4375 to 0.4375
- cotangent: bfloat16 [32, 128, 8, 2, 32], P('dp', None, 'space'), may hold values from -96 to 96
Outputs:
- pooled: bfloat16 [32, 128, 8, 2, 32], P('dp', None, 'space')
- volume_grad: bfloat16 [32, 32, 32, 8, 128], P('dp', None, 'space')
- grad_first: float32 [864, 64], P('dp')
- grad_second: float32 [1728, 128], P('dp')
The draws below stay inside these ranges and needn't reach their ends.
All inputs are finite; a program needn't handle non-finite values.
Results may differ from the reference program's by a relative error of at most 0.023.
Values may be sent and summed in bfloat16 or wider, within the bound.
A program may use at most 128 MiB of HBM per device.

```python
import jax
import jax.numpy as jnp
from jax import lax

C0 = 32
C1 = 64
C2 = 128
Y = 8
Z = 128
SAMPLES = 32
X = 32
K1 = 864
K2 = 1728


def level_of(rng, extent, cuts, low, top_value):
    loudness, own = 1.0, jax.random.fold_in(rng, 6)
    for dim, blocks in cuts:
        draws = jnp.exp(jax.random.uniform(jax.random.fold_in(own, dim), (blocks,), jnp.float32, low / len(cuts), top_value / len(cuts)))
        loudness = loudness * jnp.repeat(draws, extent[dim] // blocks).reshape([-1 if axis == dim else 1 for axis in range(len(extent))])
    return loudness


def gaussian(stream_key, dims, deviation, limit, cuts=(), kind=jnp.bfloat16):
    gain = level_of(stream_key, dims, cuts, -0.22, 0.18) if cuts else 1.0
    entries = jax.random.normal(stream_key, dims, jnp.float32) * deviation * gain
    return jnp.minimum(jnp.maximum(entries, -limit), limit).astype(kind)


def setup_inputs(seed: int = 0) -> dict:
    streams_of = jax.random.split(jax.random.key(seed), 5)
    volumes = gaussian(streams_of[0], (SAMPLES, C0, X, Y, Z), 1.0, 6.0, ((0, 32), (2, 8)))
    w_first = gaussian(streams_of[1], (K1, C1), K1 ** -0.5, 0.21875, ((0, 32),))
    w_second = gaussian(streams_of[2], (K2, C2), (K2 // 8) ** -0.5, 0.4375, ((0, 32),))
    cotangent = gaussian(streams_of[3], (SAMPLES, C2, X // 4, Y // 4, Z // 4), 16.0, 96.0, ((0, 32), (2, 8)))
    return {"volumes": volumes, "w_first": w_first, "w_second": w_second, "cotangent": cotangent}


def conv_forward(field, weight):
    in_width, extent_x, extent_y, extent_z = field.shape
    out_width = weight.shape[1]
    padded = jnp.pad(field.astype(jnp.float32), ((0, 0), (1, 1), (1, 1), (1, 1)))
    kernel = weight.astype(jnp.float32).reshape(3, 3, 3, in_width, out_width)
    summed = jnp.zeros((out_width, extent_x, extent_y, extent_z), jnp.float32)
    for along_x in range(3):
        for along_y in range(3):
            for along_z in range(3):
                window = padded[:, along_x:along_x + extent_x, along_y:along_y + extent_y, along_z:along_z + extent_z]
                summed = summed + jnp.einsum('ixyz,io->oxyz', window, kernel[along_x, along_y, along_z])
    return summed

def conv_input_grad(grads, weight, in_width):
    out_width, extent_x, extent_y, extent_z = grads.shape
    padded = jnp.pad(grads.astype(jnp.float32), ((0, 0), (1, 1), (1, 1), (1, 1)))
    kernel = weight.astype(jnp.float32).reshape(3, 3, 3, in_width, out_width)
    summed = jnp.zeros((in_width, extent_x, extent_y, extent_z), jnp.float32)
    for along_x in range(3):
        for along_y in range(3):
            for along_z in range(3):
                window = padded[:, 2 - along_x:2 - along_x + extent_x, 2 - along_y:2 - along_y + extent_y, 2 - along_z:2 - along_z + extent_z]
                summed = summed + jnp.einsum('oxyz,io->ixyz', window, kernel[along_x, along_y, along_z])
    return summed

def conv_weight_grad(field, grads):
    in_width, extent_x, extent_y, extent_z = field.shape
    padded = jnp.pad(field.astype(jnp.float32), ((0, 0), (1, 1), (1, 1), (1, 1)))
    grads_wide = grads.astype(jnp.float32)
    pieces = []
    for along_x in range(3):
        for along_y in range(3):
            for along_z in range(3):
                window = padded[:, along_x:along_x + extent_x, along_y:along_y + extent_y, along_z:along_z + extent_z]
                pieces.append(jnp.einsum('ixyz,oxyz->io', window, grads_wide))
    return jnp.stack(pieces).reshape(27 * in_width, grads.shape[0])

def pooling(field):
    width, extent_x, extent_y, extent_z = field.shape
    blocks = field.reshape(width, extent_x // 2, 2, extent_y // 2, 2, extent_z // 2, 2)
    return lax.optimization_barrier(jnp.mean(blocks, axis=(2, 4, 6)))

def spread_up(field):
    width, extent_x, extent_y, extent_z = field.shape
    blocks = jnp.broadcast_to(field[:, :, None, :, None, :, None], (width, extent_x, 2, extent_y, 2, extent_z, 2))
    return blocks.reshape(width, 2 * extent_x, 2 * extent_y, 2 * extent_z)

def silu_slope(values):
    sigma = jax.nn.sigmoid(values)
    return sigma * (1.0 + values * (1.0 - sigma))

def reference(volumes, w_first, w_second, cotangent):
    in_width = volumes.shape[1]
    mid_width = w_first.shape[1]

    def per_sample(running, sample_pair):
        volume, cotangent_one = sample_pair
        first_pre = conv_forward(volume, w_first)
        first_pool = pooling(jax.nn.silu(first_pre)).astype(jnp.bfloat16)
        second_pre = conv_forward(first_pool, w_second)
        pooled_one = pooling(jax.nn.silu(second_pre)).astype(jnp.bfloat16)
        second_delta = (spread_up(cotangent_one.astype(jnp.float32)) * 0.125 * silu_slope(second_pre)).astype(jnp.bfloat16)
        grad_two = conv_weight_grad(first_pool, second_delta)
        pool_grad = conv_input_grad(second_delta, w_second, mid_width).astype(jnp.bfloat16)
        first_delta = (spread_up(pool_grad.astype(jnp.float32)) * 0.125 * silu_slope(first_pre)).astype(jnp.bfloat16)
        grad_one = conv_weight_grad(volume, first_delta)
        input_grad = conv_input_grad(first_delta, w_first, in_width).astype(jnp.bfloat16)
        return ((running[0] + grad_one, running[1] + grad_two), (pooled_one, input_grad))
    start = (jnp.zeros(w_first.shape, jnp.float32), jnp.zeros(w_second.shape, jnp.float32))
    sums, stacked = lax.scan(per_sample, start, (volumes, cotangent))
    factor_one = float(SAMPLES * X * Y * Z) ** (-0.5)
    factor_two = float(SAMPLES * X * Y * Z // 8) ** (-0.5)
    return (stacked[0], stacked[1], sums[0] * factor_one, sums[1] * factor_two)
```

```python
import functools

import jax
import jax.numpy as jnp
from jax import lax
from jax.experimental import pallas as pl
from jax.experimental.pallas import tpu as pltpu
from jax.sharding import PartitionSpec as P

MESH = pl.DeviceIdType.MESH
F32 = jnp.float32
BF16 = jnp.bfloat16

DP = 32
SP = 8
CHIPS = 16
C0, C1, C2 = 32, 64, 128
X, Y, Z = 4, 8, 128
R1, R2 = 27, 54
FACTOR_ONE = float(1048576) ** (-0.5)
FACTOR_TWO = float(131072) ** (-0.5)


def dot(a, b):
    return lax.dot_general(a, b, (((1,), (0,)), ((), ())), preferred_element_type=F32)


def dot_nt(a, b):
    return lax.dot_general(a, b, (((1,), (1,)), ((), ())), preferred_element_type=F32)


def lanes(rows):
    return lax.broadcasted_iota(jnp.int32, (rows, Z), 1)


def shifted(tile, by):
    moved = pltpu.roll(tile, by % Z, 1)
    at = lanes(tile.shape[0])
    keep = at >= by if by > 0 else at < Z + by
    return jnp.where(keep, moved, 0.0)


def frame_plane(source, dest, rows, count, step):
    zero = jnp.zeros((3 * rows, Z), BF16)
    dest[0 : 3 * rows, 0:Z] = zero
    dest[6 * rows : 9 * rows, (count - 1) * Z : count * Z] = zero
    for y in range(count):
        tile = source[y]
        wide = tile.astype(F32)
        three = (shifted(wide, step).astype(BF16), tile, shifted(wide, -step).astype(BF16))
        for b in range(3):
            to = y - b + 1
            if 0 <= to < count:
                for c in range(3):
                    row = (b * 3 + c) * rows
                    dest[row : row + rows, to * Z : (to + 1) * Z] = three[c]


def gather_taps(parts, rows, count, y, step):
    total = None
    for c in range(3):
        column = None
        for b in range(3):
            at = y - b + 1
            if 0 <= at < count:
                row = (b * 3 + c) * rows
                piece = parts[row : row + rows, at * Z : (at + 1) * Z]
                column = piece if column is None else column + piece
        if c == 0:
            column = shifted(column, -step)
        elif c == 2:
            column = shifted(column, step)
        total = column if total is None else total + column
    return total


def kernel(
    vol, wpack, cot,
    pooled_out, vgrad_out, gone_out, gtwo_out,
    vp, s1, pre1, slope1, pp, s2, d2, d1, taps1, taps2,
    wg1, wg2, wf1, wf2, w1, w2, w1t, w2t,
    gs1, gs2, gp1, gp2, ra2, pb2, rb2, rb1, sc, rc,
    vin_sem, halo_send, halo_recv, w1_send, w1_recv, w2_send, w2_recv, wf_send, wf_recv,
    a2_send, a2_recv, b2_send, b2_recv, b1_send, b1_recv, c_send, c_recv,
):
    d = lax.axis_index("dp")
    s = lax.axis_index("space")
    core = lax.rem(d, 2)
    chip = d // 2
    sibling = chip * 2 + 1 - core

    def remote(src, dst, ssem, rsem, **where):
        return pltpu.make_async_remote_copy(
            src_ref=src, dst_ref=dst, send_sem=ssem, recv_sem=rsem,
            device_id=where, device_id_type=MESH,
        )

    barrier = pltpu.get_barrier_semaphore()

    def greet_dp(k, carry):
        pl.semaphore_signal(barrier, inc=1, device_id={"dp": lax.rem(d + k, DP)}, device_id_type=MESH)
        return carry

    def greet_space(k, carry):
        pl.semaphore_signal(barrier, inc=1, device_id={"space": lax.rem(s + k, SP)}, device_id_type=MESH)
        return carry

    vin = pltpu.make_async_copy(vol, vp.at[pl.ds(1, X)], vin_sem)
    vin.start()
    lax.fori_loop(1, DP, greet_dp, 0)
    lax.fori_loop(1, SP, greet_space, 0)
    pl.semaphore_wait(barrier, DP + SP - 2)

    def halo(n, low_src, high_src, low_dst, high_dst):
        up = remote(high_src, low_dst, halo_send.at[n, 0], halo_recv.at[n, 0], space=lax.rem(s + 1, SP))
        down = remote(low_src, high_dst, halo_send.at[n, 1], halo_recv.at[n, 1], space=lax.rem(s + SP - 1, SP))

        def start():
            @pl.when(s < SP - 1)
            def _():
                up.start()

            @pl.when(s > 0)
            def _():
                down.start()

        def wait():
            @pl.when(s > 0)
            def _():
                up.wait_recv()

            @pl.when(s == 0)
            def _():
                low_dst[...] = jnp.zeros(low_dst.shape, BF16)

            @pl.when(s < SP - 1)
            def _():
                down.wait_recv()

            @pl.when(s == SP - 1)
            def _():
                high_dst[...] = jnp.zeros(high_dst.shape, BF16)

        def drain():
            @pl.when(s < SP - 1)
            def _():
                up.wait_send()

            @pl.when(s > 0)
            def _():
                down.wait_send()

        return start, wait, drain

    def w1_copy(k):
        return remote(
            wpack.at[pl.ds(0, 16)], wg1.at[d], w1_send.at[k], w1_recv.at[k], dp=lax.rem(d + k, DP)
        )

    def w2_copy(k):
        peer = lax.rem(chip + k, CHIPS)
        return remote(
            wpack.at[pl.ds(16, 64)], wg2.at[chip, core], w2_send.at[k], w2_recv.at[k], dp=peer * 2 + core
        )

    def each(low, high, action):
        def body(k, carry):
            action(k)
            return carry

        lax.fori_loop(low, high, body, 0)

    each(1, DP, lambda k: w1_copy(k).start())
    v_start, v_wait, v_drain = halo(0, vol.at[0], vol.at[X - 1], vp.at[0], vp.at[X + 1])
    v_start()
    each(1, CHIPS, lambda k: w2_copy(k).start())
    wg1[d] = wpack[0:16]
    wg2[chip, core] = wpack[16:80]

    vin.wait()
    each(1, X + 1, lambda k: frame_plane(vp.at[k], s1.at[k], C0, Y, 1))
    v_wait()
    frame_plane(vp.at[0], s1.at[0], C0, Y, 1)
    frame_plane(vp.at[X + 1], s1.at[X + 1], C0, Y, 1)

    each(1, DP, lambda k: w1_copy(k).wait_recv())
    for k in range(DP):
        block = wg1[k].astype(F32)
        wf1[R1 * k : R1 * k + 16, 0:C1] = block[:, 0:C1]
        wf1[R1 * k + 16 : R1 * k + R1, 0:C1] = pltpu.roll(block, 64, 1)[0 : R1 - 16, 0:C1]
    w1[...] = wf1[...].astype(BF16)
    w1t[...] = wf1[...].T.astype(BF16)

    def first_layer(h):
        for k in range(2):
            x = 2 * h + k
            pre1[k] = dot(w1t[...], s1[pl.ds(x, 3)].reshape(27 * C0, Y * Z))
        even = lax.rem(lanes(C1), 2) == 0
        for y in range(Y // 2):
            total = jnp.zeros((C1, Z), F32)
            for k in range(2):
                for j in range(2):
                    at = slice((2 * y + j) * Z, (2 * y + j + 1) * Z)
                    t = pre1[k, :, at]
                    sigma = jax.nn.sigmoid(t)
                    total = total + t * sigma
                    slope1[2 * h + k, :, at] = sigma * (1.0 + t * (1.0 - sigma)) * 0.125
            other = jnp.where(even, pltpu.roll(total, Z - 1, 1), pltpu.roll(total, 1, 1))
            pp[h + 1, y] = ((total + other) * 0.125).astype(BF16)

    each(0, 2, first_layer)
    p_start, p_wait, p_drain = halo(1, pp.at[1], pp.at[2], pp.at[0], pp.at[3])
    p_start()

    each(1, CHIPS, lambda k: w2_copy(k).wait_recv())
    forward = remote(wg2.at[:, core], wg2.at[:, core], wf_send, wf_recv, dp=sibling)
    forward.start()
    each(1, 3, lambda k: frame_plane(pp.at[k], s2.at[k], C1, Y // 2, 2))
    forward.wait_recv()
    for k in range(DP):
        wf2[R2 * k : R2 * k + R2, :] = wg2[k // 2, k % 2].astype(F32)[0:R2]
    w2[...] = wf2[...].astype(BF16)
    w2t[...] = wf2[...].T.astype(BF16)
    p_wait()
    frame_plane(pp.at[0], s2.at[0], C1, Y // 2, 2)
    frame_plane(pp.at[3], s2.at[3], C1, Y // 2, 2)

    spread = jnp.where(
        lax.broadcasted_iota(jnp.int32, (32, Z), 1) // 4 == lax.broadcasted_iota(jnp.int32, (32, Z), 0), 1.0, 0.0
    ).astype(BF16)
    squeeze = jnp.where(
        lax.broadcasted_iota(jnp.int32, (Z, 32), 0) // 4 == lax.broadcasted_iota(jnp.int32, (Z, 32), 1), 0.5, 0.0
    ).astype(BF16)
    for x in range(2):
        taps2[0:C2, x * 512 : (x + 1) * 512] = dot(w2t[...], s2[x : x + 3].reshape(27 * C1, Y // 2 * Z))
    for y in range(2):
        spreaded = dot(cot[y], spread) * 0.125
        total = jnp.zeros((C2, Z), F32)
        for x in range(2):
            for j in range(2):
                yy = 2 * y + j
                t = taps2[0:C2, x * 512 + yy * Z : x * 512 + (yy + 1) * Z]
                sigma = jax.nn.sigmoid(t)
                total = total + t * sigma
                d2[x + 1, :, yy * Z : (yy + 1) * Z] = (
                    spreaded * (sigma * (1.0 + t * (1.0 - sigma)))
                ).astype(BF16)
        total = total * 0.125
        high = total.astype(BF16)
        low = (total - high.astype(F32)).astype(BF16)
        pooled_out[y] = (dot(high, squeeze) + dot(low, squeeze)).astype(BF16)
    e_start, e_wait, e_drain = halo(2, d2.at[1], d2.at[2], d2.at[0], d2.at[3])
    e_start()

    for a in range(3):
        gs2[a * 576 : (a + 1) * 576, :] = (
            dot_nt(s2[a], d2[1]) + dot_nt(s2[a + 1], d2[2])
        )
    for k in range(DP):
        gp2[k // 2, k % 2, 0:R2, :] = gs2[R2 * k : R2 * k + R2, :].astype(BF16)
        gp2[k // 2, k % 2, R2:64, :] = jnp.zeros((64 - R2, C2), BF16)
    pair = remote(gp2.at[:, 1 - core], ra2, a2_send, a2_recv, dp=sibling)
    pair.start()

    e_wait()
    left2 = jnp.concatenate([w2[1152:1728], w2[576:1152], w2[0:576]], axis=1)
    for x in range(2):
        taps2[:, 0:512] = dot(left2, d2[x : x + 3].reshape(3 * C2, 512))
        for y in range(Y // 2):
            grad = gather_taps(taps2, C1, Y // 2, y, 2).astype(BF16).astype(F32)
            for k in range(2):
                for j in range(2):
                    at = slice((2 * y + j) * Z, (2 * y + j + 1) * Z)
                    d1[2 * x + k + 1, :, at] = (grad * slope1[2 * x + k, :, at]).astype(BF16)
    f_start, f_wait, f_drain = halo(3, d1.at[1], d1.at[X], d1.at[0], d1.at[X + 1])
    f_start()

    pair.wait_recv()

    def add_pair(k):
        pb2[k] = (gp2[k, core].astype(F32) + ra2[k].astype(F32)).astype(BF16)

    each(0, CHIPS, add_pair)

    def b2_copy(k):
        peer = lax.rem(chip + k, CHIPS)
        return remote(pb2.at[peer], rb2.at[k], b2_send.at[k], b2_recv.at[k], dp=peer * 2 + core)

    each(1, CHIPS, lambda k: b2_copy(k).start())

    for a in range(3):
        acc = dot_nt(s1[a], d1[1])
        for x in range(1, X):
            acc = acc + dot_nt(s1[a + x], d1[x + 1])
        gs1[a * 288 : (a + 1) * 288, :] = acc
    for k in range(DP):
        head = gs1[R1 * k : R1 * k + 16, :].astype(BF16)
        tail = jnp.concatenate(
            [gs1[R1 * k + 16 : R1 * k + R1, :], jnp.zeros((32 - R1, C1), F32)], axis=0
        ).astype(BF16)
        gp1[k] = jnp.concatenate([head, tail], axis=1)

    def b1_copy(k):
        peer = lax.rem(d + k, DP)
        return remote(gp1.at[peer], rb1.at[k], b1_send.at[k], b1_recv.at[k], dp=peer)

    each(1, DP, lambda k: b1_copy(k).start())

    f_wait()
    left1 = jnp.concatenate([w1[576:864], w1[288:576], w1[0:288]], axis=1)

    def volume_grad(x):
        taps1[...] = dot(left1, d1[pl.ds(x, 3)].reshape(3 * C1, Y * Z))
        for y in range(Y):
            vgrad_out[x, y] = gather_taps(taps1, C0, Y, y, 1).astype(BF16)

    each(0, X, volume_grad)

    each(1, CHIPS, lambda k: b2_copy(k).wait_recv())
    sum2 = lax.fori_loop(1, CHIPS, lambda k, t: t + rb2[k].astype(F32), pb2[chip].astype(F32))
    sc[16:80] = sum2.astype(BF16)
    each(1, DP, lambda k: b1_copy(k).wait_recv())
    sum1 = lax.fori_loop(1, DP, lambda k, t: t + rb1[k].astype(F32), gp1[d].astype(F32))
    sc[0:16] = sum1.astype(BF16)

    def c_copy(k):
        return remote(sc, rc.at[k], c_send.at[k], c_recv.at[k], space=lax.rem(s + k, SP))

    each(1, SP, lambda k: c_copy(k).start())
    each(1, SP, lambda k: c_copy(k).wait_recv())
    full = lax.fori_loop(1, SP, lambda k, t: t + rc[k].astype(F32), sc[...].astype(F32))
    gtwo_out[...] = full[16 : 16 + R2] * (0.5 * FACTOR_TWO)
    gone_out[0:16, :] = full[0:16, 0:C1] * FACTOR_ONE
    gone_out[16:R1, :] = pltpu.roll(full[0:16], 64, 1)[0 : R1 - 16, 0:C1] * FACTOR_ONE

    v_drain()
    p_drain()
    e_drain()
    f_drain()
    each(1, DP, lambda k: w1_copy(k).wait_send())
    each(1, CHIPS, lambda k: w2_copy(k).wait_send())
    forward.wait_send()
    pair.wait_send()
    each(1, CHIPS, lambda k: b2_copy(k).wait_send())
    each(1, DP, lambda k: b1_copy(k).wait_send())
    each(1, SP, lambda k: c_copy(k).wait_send())


def local(volumes, w_first, w_second, cotangent):
    vol = volumes[0].transpose(1, 2, 0, 3)
    head = jnp.concatenate([w_first[0:16], jnp.pad(w_first[16:R1], ((0, 32 - R1), (0, 0)))], axis=1)
    wpack = jnp.concatenate([head, jnp.pad(w_second, ((0, 64 - R2), (0, 0)))], axis=0)
    cot = cotangent[0, :, 0].transpose(1, 0, 2)
    vmem = pl.BlockSpec(memory_space=pltpu.VMEM)
    dma = pltpu.SemaphoreType.DMA
    pooled, vgrad, gone, gtwo = pl.pallas_call(
        kernel,
        out_shape=(
            jax.ShapeDtypeStruct((2, C2, 32), BF16),
            jax.ShapeDtypeStruct((X, Y, C0, Z), BF16),
            jax.ShapeDtypeStruct((R1, C1), F32),
            jax.ShapeDtypeStruct((R2, C2), F32),
        ),
        in_specs=[pl.BlockSpec(memory_space=pl.ANY), vmem, vmem],
        out_specs=(vmem, vmem, vmem, vmem),
        scratch_shapes=[
            pltpu.VMEM((X + 2, Y, C0, Z), BF16),
            pltpu.VMEM((X + 2, 9 * C0, Y * Z), BF16),
            pltpu.VMEM((2, C1, Y * Z), F32),
            pltpu.VMEM((X, C1, Y * Z), F32),
            pltpu.VMEM((4, Y // 2, C1, Z), BF16),
            pltpu.VMEM((4, 9 * C1, Y // 2 * Z), BF16),
            pltpu.VMEM((4, C2, Y // 2 * Z), BF16),
            pltpu.VMEM((X + 2, C1, Y * Z), BF16),
            pltpu.VMEM((9 * C0, Y * Z), F32),
            pltpu.VMEM((9 * C1, Y * Z), F32),
            pltpu.VMEM((DP, 16, 128), BF16),
            pltpu.VMEM((CHIPS, 2, 64, 128), BF16),
            pltpu.VMEM((27 * C0, C1), F32),
            pltpu.VMEM((27 * C1, C2), F32),
            pltpu.VMEM((27 * C0, C1), BF16),
            pltpu.VMEM((27 * C1, C2), BF16),
            pltpu.VMEM((C1, 27 * C0), BF16),
            pltpu.VMEM((C2, 27 * C1), BF16),
            pltpu.VMEM((27 * C0, C1), F32),
            pltpu.VMEM((27 * C1, C2), F32),
            pltpu.VMEM((DP, 16, 128), BF16),
            pltpu.VMEM((CHIPS, 2, 64, 128), BF16),
            pltpu.VMEM((CHIPS, 64, 128), BF16),
            pltpu.VMEM((CHIPS, 64, 128), BF16),
            pltpu.VMEM((CHIPS, 64, 128), BF16),
            pltpu.VMEM((DP, 16, 128), BF16),
            pltpu.VMEM((80, 128), BF16),
            pltpu.VMEM((SP, 80, 128), BF16),
            dma,
            dma((4, 2)), dma((4, 2)),
            dma((DP,)), dma((DP,)),
            dma((CHIPS,)), dma((CHIPS,)),
            dma, dma,
            dma, dma,
            dma((CHIPS,)), dma((CHIPS,)),
            dma((DP,)), dma((DP,)),
            dma((SP,)), dma((SP,)),
        ],
        compiler_params=pltpu.CompilerParams(
            collective_id=0, has_side_effects=True, vmem_limit_bytes=48 * 1024 * 1024
        ),
    )(vol, wpack, cot)
    return (
        pooled.transpose(1, 0, 2)[None, :, None],
        vgrad.transpose(2, 0, 1, 3)[None],
        gone,
        gtwo,
    )


def solution(mesh):
    return jax.shard_map(
        local,
        mesh=mesh,
        in_specs=(
            P("dp", None, "space", None, None),
            P("dp", None),
            P("dp", None),
            P("dp", None, "space", None, None),
        ),
        out_specs=(
            P("dp", None, "space", None, None),
            P("dp", None, "space", None, None),
            P("dp", None),
            P("dp", None),
        ),
        check_vma=False,
    )
```

```python
import functools

import jax
import jax.numpy as jnp
from jax import lax
from jax.experimental import pallas as pl
from jax.experimental.pallas import tpu as pltpu
from jax.sharding import PartitionSpec as P

MESH = pl.DeviceIdType.MESH
F32 = jnp.float32
BF16 = jnp.bfloat16

DP = 32
SP = 8
CHIPS = 16
C0, C1, C2 = 32, 64, 128
X, Y, Z = 4, 8, 128
R1, R2 = 27, 54
VMEM_BYTES = 56 * 1024 * 1024
FACTOR_ONE = float(1048576) ** (-0.5)
FACTOR_TWO = float(131072) ** (-0.5)


def dot(a, b):
    return lax.dot_general(a, b, (((1,), (0,)), ((), ())), preferred_element_type=F32)


def dot_nt(a, b):
    return lax.dot_general(a, b, (((1,), (1,)), ((), ())), preferred_element_type=F32)


def lanes(rows):
    return lax.broadcasted_iota(jnp.int32, (rows, Z), 1)


def shifted(tile, by):
    moved = pltpu.roll(tile, by % Z, 1)
    at = lanes(tile.shape[0])
    keep = at >= by if by > 0 else at < Z + by
    return jnp.where(keep, moved, 0.0)


def frame_plane(source, dest, rows, count, step):
    zero = jnp.zeros((3 * rows, Z), BF16)
    dest[0 : 3 * rows, 0:Z] = zero
    dest[6 * rows : 9 * rows, (count - 1) * Z : count * Z] = zero
    for y in range(count):
        wide = source(y)
        three = [t.astype(BF16) for t in (shifted(wide, step), wide, shifted(wide, -step))]
        for b in range(3):
            to = y - b + 1
            if 0 <= to < count:
                for c in range(3):
                    row = (b * 3 + c) * rows
                    dest[row : row + rows, to * Z : (to + 1) * Z] = three[c]


def gather_taps(parts, rows, count, y, step):
    total = None
    for c in range(3):
        column = None
        for b in range(3):
            at = y - b + 1
            if 0 <= at < count:
                row = (b * 3 + c) * rows
                piece = parts[row : row + rows, at * Z : (at + 1) * Z]
                column = piece if column is None else column + piece
        if c == 0:
            column = shifted(column, -step)
        elif c == 2:
            column = shifted(column, step)
        total = column if total is None else total + column
    return total


def kernel(
    vol_in, wone_in, wtwo_in, cot_in,
    pooled_to, vgrad_to, gone_to, gtwo_to,
    pooled_out, vgrad_out, gone_out, gtwo_out, vol, wone, wtwo, cot, vh, fst, s1, pre1, slope1, pp, ps, ph, s2, pre2, d2, es, eh, d1, taps1, taps2, fs, fh,
    wpad, wsend, wg1, wg2, wf1, wf2, w1, w2, w1t, w2t,
    gs1, gs2, gp1, gp2, ra1, ra2, pb1, pb2, rb1, rb2, sc1, sc2, rc1, rc2,
    in_sem, out_sem, halo_send, halo_recv, pair_send, pair_recv,
    w1_send, w1_recv, w2_send, w2_recv,
    b1_send, b1_recv, b2_send, b2_recv, c1_send, c1_recv, c2_send, c2_recv,
):
    d = lax.axis_index("dp")
    s = lax.axis_index("space")
    core = lax.rem(d, 2)
    chip = d // 2
    sibling = chip * 2 + 1 - core

    def remote(src, dst, ssem, rsem, **where):
        return pltpu.make_async_remote_copy(
            src_ref=src, dst_ref=dst, send_sem=ssem, recv_sem=rsem,
            device_id=where, device_id_type=MESH,
        )

    def each(low, high, action):
        def body(k, carry):
            action(k)
            return carry

        lax.fori_loop(low, high, body, 0)

    def peer(k):
        return lax.rem(chip + k, CHIPS) * 2 + core

    def greet(**where):
        pl.semaphore_signal(barrier, inc=1, device_id=where, device_id_type=MESH)

    barrier = pltpu.get_barrier_semaphore()
    loads = [
        pltpu.make_async_copy(src, dst, in_sem.at[k])
        for k, (src, dst) in enumerate(((wone_in, wone), (wtwo_in, wtwo), (vol_in, vol), (cot_in, cot)))
    ]
    for load in loads:
        load.start()
    each(1, CHIPS, lambda k: greet(dp=peer(k)))
    each(1, SP, lambda k: greet(space=lax.rem(s + k, SP)))
    greet(dp=sibling)

    loads[0].wait()
    loads[1].wait()
    wpad[0:R1] = wone[...].astype(F32)
    wpad[R1:32] = jnp.zeros((32 - R1, C1), F32)
    wsend[0:16] = jnp.concatenate([wpad[0:16], wpad[16:32]], axis=1).astype(BF16)
    wsend[16 : 16 + R2] = wtwo[...]
    wsend[16 + R2 : 80] = jnp.zeros((64 - R2, C2), BF16)
    wg1[chip, core] = wsend[0:16]
    wg2[chip, core] = wsend[16:80]
    loads[2].wait()
    for k in range(2):
        vh[k] = vol[0, :, 0 if k == 0 else X - 1]
    pl.semaphore_wait(barrier, CHIPS - 1 + SP - 1 + 1)

    def halo(n, low_src, high_src, low_dst, high_dst):
        up = remote(high_src, low_dst, halo_send.at[n, 0], halo_recv.at[n, 0], space=lax.rem(s + 1, SP))
        down = remote(low_src, high_dst, halo_send.at[n, 1], halo_recv.at[n, 1], space=lax.rem(s + SP - 1, SP))

        def start():
            @pl.when(s < SP - 1)
            def _():
                up.start()

            @pl.when(s > 0)
            def _():
                down.start()

        def wait():
            @pl.when(s > 0)
            def _():
                up.wait_recv()

            @pl.when(s == 0)
            def _():
                low_dst[...] = jnp.zeros(low_dst.shape, BF16)

            @pl.when(s < SP - 1)
            def _():
                down.wait_recv()

            @pl.when(s == SP - 1)
            def _():
                high_dst[...] = jnp.zeros(high_dst.shape, BF16)

        def drain():
            @pl.when(s < SP - 1)
            def _():
                up.wait_send()

            @pl.when(s > 0)
            def _():
                down.wait_send()

        return start, wait, drain

    def w1_copy(k):
        return remote(wsend.at[pl.ds(0, 16)], wg1.at[chip, core], w1_send.at[k], w1_recv.at[k], dp=peer(k))

    def w2_copy(k):
        return remote(wsend.at[pl.ds(16, 64)], wg2.at[chip, core], w2_send.at[k], w2_recv.at[k], dp=peer(k))

    each(1, CHIPS, lambda k: w1_copy(k).start())
    v_start, v_wait, v_drain = halo(0, vh.at[0], vh.at[1], vh.at[2], vh.at[3])
    v_start()
    each(1, CHIPS, lambda k: w2_copy(k).start())

    def frame_input(plane, dest):
        fst[...] = plane.astype(F32).reshape(C0 * Y, Z)
        frame_plane(lambda y: fst[pl.ds(y, C0, stride=Y), :], dest, C0, Y, 1)

    each(0, X, lambda k: frame_input(vol[0, :, k], s1.at[k + 1]))

    each(1, CHIPS, lambda k: w1_copy(k).wait_recv())
    forward1 = remote(wg1.at[:, core], wg1.at[:, core], pair_send.at[0], pair_recv.at[0], dp=sibling)
    forward1.start()
    v_wait()
    each(0, 2, lambda k: frame_input(vh[k + 2], s1.at[k * (X + 1)]))
    forward1.wait_recv()
    for k in range(DP):
        block = wg1[k // 2, k % 2].astype(F32)
        wf1[R1 * k : R1 * k + 16, 0:C1] = block[:, 0:C1]
        wf1[R1 * k + 16 : R1 * k + R1, 0:C1] = pltpu.roll(block, 64, 1)[0 : R1 - 16, 0:C1]
    w1[...] = wf1[...].astype(BF16)
    w1t[...] = wf1[...].T.astype(BF16)

    even = lax.rem(lanes(C1), 2) == 0

    def first_layer(h):
        for k in range(2):
            x = 2 * h + k
            pre1[k] = dot(w1t[...], s1[pl.ds(x, 3)].reshape(27 * C0, Y * Z))
        for y in range(Y // 2):
            total = jnp.zeros((C1, Z), F32)
            for k in range(2):
                for j in range(2):
                    at = slice((2 * y + j) * Z, (2 * y + j + 1) * Z)
                    t = pre1[k, :, at]
                    sigma = jax.nn.sigmoid(t)
                    total = total + t * sigma
                    slope1[2 * h + k, :, at] = sigma * (1.0 + t * (1.0 - sigma)) * 0.125
            other = jnp.where(even, pltpu.roll(total, Z - 1, 1), pltpu.roll(total, 1, 1))
            pp[h, y] = (total + other) * 0.125

    each(0, 2, first_layer)
    for h in range(2):
        for y in range(2):
            ps[h, y] = jnp.where(even, pp[h, 2 * y], pp[h, 2 * y + 1]).astype(BF16)
    p_start, p_wait, p_drain = halo(1, ps.at[0], ps.at[1], ph.at[0], ph.at[1])
    p_start()

    def apart(pairs, y):
        wide = pairs[y // 2].astype(F32)
        if y % 2 == 0:
            return jnp.where(even, wide, pltpu.roll(wide, 1, 1))
        return jnp.where(even, pltpu.roll(wide, Z - 1, 1), wide)

    each(1, CHIPS, lambda k: w2_copy(k).wait_recv())
    forward2 = remote(wg2.at[:, core], wg2.at[:, core], pair_send.at[1], pair_recv.at[1], dp=sibling)
    forward2.start()
    for h in range(2):
        frame_plane(lambda y: pp[h, y], s2.at[h + 1], C1, Y // 2, 2)
    forward2.wait_recv()
    for k in range(DP):
        wf2[R2 * k : R2 * k + R2, :] = wg2[k // 2, k % 2].astype(F32)[0:R2]
    w2[...] = wf2[...].astype(BF16)
    w2t[...] = wf2[...].T.astype(BF16)
    p_wait()
    for h in range(2):
        frame_plane(lambda y: apart(ph[h], y), s2.at[3 * h], C1, Y // 2, 2)

    loads[3].wait()
    spread = jnp.where(
        lax.broadcasted_iota(jnp.int32, (32, Z), 1) // 4 == lax.broadcasted_iota(jnp.int32, (32, Z), 0), 1.0, 0.0
    ).astype(BF16)
    squeeze = jnp.where(
        lax.broadcasted_iota(jnp.int32, (32, Z), 1) // 4 == lax.broadcasted_iota(jnp.int32, (32, Z), 0), 0.5, 0.0
    ).astype(BF16)
    for x in range(2):
        pre2[x] = dot(w2t[...], s2[x : x + 3].reshape(27 * C1, Y // 2 * Z))
    sums = []
    for y in range(2):
        spreaded = lax.dot_general(cot[y], spread, (((0,), (0,)), ((), ())), preferred_element_type=F32) * 0.125
        total = jnp.zeros((C2, Z), F32)
        for x in range(2):
            for j in range(2):
                at = slice((2 * y + j) * Z, (2 * y + j + 1) * Z)
                t = pre2[x, :, at]
                sigma = jax.nn.sigmoid(t)
                total = total + t * sigma
                d2[x, :, at] = (spreaded * (sigma * (1.0 + t * (1.0 - sigma)))).astype(BF16)
        sums.append(total)

    for k in range(2):
        taps2[0:576] = dot(w2[1152 * k : 1152 * k + 576], d2[k])
        for y in range(2):
            a, b = (gather_taps(taps2, C1, Y // 2, 2 * y + j, 2) for j in range(2))
            es[k, y] = jnp.where(even, a, b).astype(BF16)
    e_start, e_wait, e_drain = halo(2, es.at[0], es.at[1], eh.at[0], eh.at[1])
    e_start()

    for a in range(3):
        gs2[a * 576 : (a + 1) * 576, :] = dot_nt(s2[a], d2[0]) + dot_nt(s2[a + 1], d2[1])
    for k in range(DP):
        gp2[k // 2, k % 2, 0:R2, :] = gs2[R2 * k : R2 * k + R2, :].astype(BF16)
        gp2[k // 2, k % 2, R2:64, :] = jnp.zeros((64 - R2, C2), BF16)
    pair2 = remote(gp2.at[:, 1 - core], ra2, pair_send.at[2], pair_recv.at[2], dp=sibling)
    pair2.start()

    for x in range(2):
        left = jnp.concatenate([w2[(x + 1) * 576 : (x + 2) * 576], w2[x * 576 : (x + 1) * 576]], axis=1)
        taps2[x * 576 : (x + 1) * 576] = dot(left, d2[...].reshape(2 * C2, Y // 2 * Z))

    for y in range(2):
        total = sums[y] * 0.125
        high = total.astype(BF16)
        low = (total - high.astype(F32)).astype(BF16)
        pooled_out[y] = (dot_nt(squeeze, high) + dot_nt(squeeze, low)).astype(BF16)
    store_pooled = pltpu.make_async_copy(pooled_out, pooled_to, out_sem.at[X])
    store_pooled.start()

    pair2.wait_recv()

    def add_pair2(k):
        pb2[k] = (gp2[k, core].astype(F32) + ra2[k].astype(F32)).astype(BF16)

    each(0, CHIPS, add_pair2)

    def b2_copy(k):
        return remote(
            pb2.at[lax.rem(chip + k, CHIPS)], rb2.at[k], b2_send.at[k], b2_recv.at[k], dp=peer(k)
        )

    each(1, CHIPS, lambda k: b2_copy(k).start())

    e_wait()
    for k in range(2):
        d1[k] = jnp.zeros((C1, Y * Z), BF16)
        d1[X + 2 + k] = jnp.zeros((C1, Y * Z), BF16)
    for x in range(2):
        for y in range(Y // 2):
            grad = gather_taps(taps2.at[x * 576 : (x + 1) * 576], C1, Y // 2, y, 2) + apart(eh[x], y)
            grad = grad.astype(BF16).astype(F32)
            for k in range(2):
                for j in range(2):
                    at = slice((2 * y + j) * Z, (2 * y + j + 1) * Z)
                    d1[2 * x + k + 2, :, at] = (grad * slope1[2 * x + k, :, at]).astype(BF16)

    def add_plane(k, acc):
        return acc + dot_nt(s1[k], d1[pl.ds(k, 3)].reshape(3 * C1, Y * Z))

    acc = lax.fori_loop(0, X + 2, add_plane, jnp.zeros((9 * C0, 3 * C1), F32))
    for a in range(3):
        gs1[a * 288 : (a + 1) * 288, :] = acc[:, (2 - a) * C1 : (3 - a) * C1]
    for k in range(DP):
        head = gs1[R1 * k : R1 * k + 16, :].astype(BF16)
        tail = jnp.concatenate(
            [gs1[R1 * k + 16 : R1 * k + R1, :], jnp.zeros((32 - R1, C1), F32)], axis=0
        ).astype(BF16)
        gp1[k // 2, k % 2] = jnp.concatenate([head, tail], axis=1)
    pair1 = remote(gp1.at[:, 1 - core], ra1, pair_send.at[3], pair_recv.at[3], dp=sibling)
    pair1.start()

    for k in range(2):
        taps1[...] = dot(w1[576 * k : 576 * k + 288], d1[2 + (X - 1) * k])
        for y in range(Y):
            fs[k, y] = gather_taps(taps1, C0, Y, y, 1).astype(BF16)
    f_start, f_wait, f_drain = halo(3, fs.at[0], fs.at[1], fh.at[0], fh.at[1])
    f_start()

    pair1.wait_recv()

    def add_pair1(k):
        pb1[k] = (gp1[k, core].astype(F32) + ra1[k].astype(F32)).astype(BF16)

    each(0, CHIPS, add_pair1)

    def b1_copy(k):
        return remote(
            pb1.at[lax.rem(chip + k, CHIPS)], rb1.at[k], b1_send.at[k], b1_recv.at[k], dp=peer(k)
        )

    each(1, CHIPS, lambda k: b1_copy(k).start())

    left1 = jnp.concatenate([w1[576:864], w1[288:576], w1[0:288]], axis=1)

    def store_vgrad(x):
        return pltpu.make_async_copy(vgrad_out.at[x], vgrad_to.at[0, :, x], out_sem.at[x])

    def volume_grad(x, extra=None):
        taps1[...] = dot(left1, d1[pl.ds(x + 1, 3)].reshape(3 * C1, Y * Z))
        for y in range(Y):
            piece = gather_taps(taps1, C0, Y, y, 1)
            if extra is not None:
                piece = piece + extra[y].astype(F32)
            fst[pl.ds(y, C0, stride=Y), :] = piece
        vgrad_out[x] = fst[...].reshape(C0, Y, Z).astype(BF16)
        store_vgrad(x).start()

    each(1, X - 1, volume_grad)
    each(1, CHIPS, lambda k: b2_copy(k).wait_recv())
    sum2 = lax.fori_loop(1, CHIPS, lambda k, t: t + rb2[k].astype(F32), pb2[chip].astype(F32))
    sc2[...] = sum2.astype(BF16)

    def c2_copy(k):
        return remote(sc2, rc2.at[k], c2_send.at[k], c2_recv.at[k], space=lax.rem(s + k, SP))

    each(1, SP, lambda k: c2_copy(k).start())
    f_wait()
    each(0, 2, lambda k: volume_grad((X - 1) * k, fh.at[k]))

    each(1, CHIPS, lambda k: b1_copy(k).wait_recv())
    sum1 = lax.fori_loop(1, CHIPS, lambda k, t: t + rb1[k].astype(F32), pb1[chip].astype(F32))
    sc1[...] = sum1.astype(BF16)

    def c1_copy(k):
        return remote(sc1, rc1.at[k], c1_send.at[k], c1_recv.at[k], space=lax.rem(s + k, SP))

    each(1, SP, lambda k: c1_copy(k).start())
    each(1, SP, lambda k: c2_copy(k).wait_recv())
    full2 = lax.fori_loop(1, SP, lambda k, t: t + rc2[k].astype(F32), sc2[...].astype(F32))
    gtwo_out[...] = full2[0:R2] * (0.5 * FACTOR_TWO)
    store_gtwo = pltpu.make_async_copy(gtwo_out, gtwo_to, out_sem.at[X + 1])
    store_gtwo.start()

    v_drain()
    p_drain()
    e_drain()
    f_drain()
    each(1, CHIPS, lambda k: w1_copy(k).wait_send())
    each(1, CHIPS, lambda k: w2_copy(k).wait_send())
    each(1, CHIPS, lambda k: b2_copy(k).wait_send())
    each(1, CHIPS, lambda k: b1_copy(k).wait_send())
    forward1.wait_send()
    forward2.wait_send()
    pair1.wait_send()
    pair2.wait_send()
    each(1, SP, lambda k: c2_copy(k).wait_send())
    each(1, SP, lambda k: c1_copy(k).wait_send())

    each(1, SP, lambda k: c1_copy(k).wait_recv())
    full1 = lax.fori_loop(1, SP, lambda k, t: t + rc1[k].astype(F32), sc1[...].astype(F32))
    gone_out[0:16, :] = full1[:, 0:C1] * FACTOR_ONE
    gone_out[16:R1, :] = pltpu.roll(full1, 64, 1)[0 : R1 - 16, 0:C1] * FACTOR_ONE
    store_gone = pltpu.make_async_copy(gone_out, gone_to, out_sem.at[X + 2])
    store_gone.start()
    each(0, X, lambda k: store_vgrad(k).wait())
    store_pooled.wait()
    store_gtwo.wait()
    store_gone.wait()


def hand_over(*refs):
    sources, dests, held, sem = refs[0:4], refs[4:8], refs[8:12], refs[12]
    loads = [pltpu.make_async_copy(sources[k], held[k], sem.at[0, k]) for k in range(4)]
    stores = [pltpu.make_async_copy(held[k], dests[k], sem.at[1, k]) for k in range(4)]
    for load in loads:
        load.start()
    for load, store in zip(loads, stores):
        load.wait()
        store.start()
    for store in stores:
        store.wait()


def local(volumes, w_first, w_second, cotangent):
    cot = cotangent[0, :, 0].transpose(1, 2, 0)
    hbm = pl.BlockSpec(memory_space=pltpu.HBM)
    shapes = (
        jax.ShapeDtypeStruct((2, 32, C2), BF16),
        jax.ShapeDtypeStruct((1, C0, X, Y, Z), BF16),
        jax.ShapeDtypeStruct((R1, C1), F32),
        jax.ShapeDtypeStruct((R2, C2), F32),
    )
    dma = pltpu.SemaphoreType.DMA
    results = pl.pallas_call(
        kernel,
        out_shape=shapes,
        in_specs=[hbm] * 4,
        out_specs=(hbm,) * 4,
        scratch_shapes=[
            pltpu.VMEM((2, 32, C2), BF16),
            pltpu.VMEM((X, C0, Y, Z), BF16),
            pltpu.VMEM((R1, C1), F32),
            pltpu.VMEM((R2, C2), F32),
            pltpu.VMEM((1, C0, X, Y, Z), BF16),
            pltpu.VMEM((R1, C1), BF16),
            pltpu.VMEM((R2, C2), BF16),
            pltpu.VMEM((2, 32, C2), BF16),
            pltpu.VMEM((4, C0, Y, Z), BF16),
            pltpu.VMEM((C0 * Y, Z), F32),
            pltpu.VMEM((X + 2, 9 * C0, Y * Z), BF16),
            pltpu.VMEM((2, C1, Y * Z), F32),
            pltpu.VMEM((X, C1, Y * Z), F32),
            pltpu.VMEM((2, Y // 2, C1, Z), F32),
            pltpu.VMEM((2, 2, C1, Z), BF16),
            pltpu.VMEM((2, 2, C1, Z), BF16),
            pltpu.VMEM((4, 9 * C1, Y // 2 * Z), BF16),
            pltpu.VMEM((2, C2, Y // 2 * Z), F32),
            pltpu.VMEM((2, C2, Y // 2 * Z), BF16),
            pltpu.VMEM((2, 2, C1, Z), BF16),
            pltpu.VMEM((2, 2, C1, Z), BF16),
            pltpu.VMEM((X + 4, C1, Y * Z), BF16),
            pltpu.VMEM((9 * C0, Y * Z), F32),
            pltpu.VMEM((18 * C1, Y // 2 * Z), F32),
            pltpu.VMEM((2, Y, C0, Z), BF16),
            pltpu.VMEM((2, Y, C0, Z), BF16),
            pltpu.VMEM((32, C1), F32),
            pltpu.VMEM((80, 128), BF16),
            pltpu.VMEM((CHIPS, 2, 16, 128), BF16),
            pltpu.VMEM((CHIPS, 2, 64, 128), BF16),
            pltpu.VMEM((27 * C0, C1), F32),
            pltpu.VMEM((27 * C1, C2), F32),
            pltpu.VMEM((27 * C0, C1), BF16),
            pltpu.VMEM((27 * C1, C2), BF16),
            pltpu.VMEM((C1, 27 * C0), BF16),
            pltpu.VMEM((C2, 27 * C1), BF16),
            pltpu.VMEM((27 * C0, C1), F32),
            pltpu.VMEM((27 * C1, C2), F32),
            pltpu.VMEM((CHIPS, 2, 16, 128), BF16),
            pltpu.VMEM((CHIPS, 2, 64, 128), BF16),
            pltpu.VMEM((CHIPS, 16, 128), BF16),
            pltpu.VMEM((CHIPS, 64, 128), BF16),
            pltpu.VMEM((CHIPS, 16, 128), BF16),
            pltpu.VMEM((CHIPS, 64, 128), BF16),
            pltpu.VMEM((CHIPS, 16, 128), BF16),
            pltpu.VMEM((CHIPS, 64, 128), BF16),
            pltpu.VMEM((16, 128), BF16),
            pltpu.VMEM((64, 128), BF16),
            pltpu.VMEM((SP, 16, 128), BF16),
            pltpu.VMEM((SP, 64, 128), BF16),
            dma((4,)), dma((X + 3,)),
            dma((4, 2)), dma((4, 2)),
            dma((4,)), dma((4,)),
            dma((CHIPS,)), dma((CHIPS,)),
            dma((CHIPS,)), dma((CHIPS,)),
            dma((CHIPS,)), dma((CHIPS,)),
            dma((CHIPS,)), dma((CHIPS,)),
            dma((SP,)), dma((SP,)),
            dma((SP,)), dma((SP,)),
        ],
        compiler_params=pltpu.CompilerParams(
            collective_id=0, has_side_effects=True, vmem_limit_bytes=VMEM_BYTES
        ),
    )(volumes, w_first, w_second, cot)
    pooled, vgrad, gone, gtwo = pl.pallas_call(
        hand_over,
        out_shape=shapes,
        in_specs=[hbm] * 4,
        out_specs=(hbm,) * 4,
        scratch_shapes=[*(pltpu.VMEM(each.shape, each.dtype) for each in shapes), dma((2, 4))],
        compiler_params=pltpu.CompilerParams(vmem_limit_bytes=VMEM_BYTES),
    )(*results)
    return (pooled.transpose(2, 0, 1)[None, :, None], vgrad, gone, gtwo)


def solution(mesh):
    return jax.shard_map(
        local,
        mesh=mesh,
        in_specs=(
            P("dp", None, "space", None, None),
            P("dp", None),
            P("dp", None),
            P("dp", None, "space", None, None),
        ),
        out_specs=(
            P("dp", None, "space", None, None),
            P("dp", None, "space", None, None),
            P("dp", None),
            P("dp", None),
        ),
        check_vma=False,
    )
```

```python
import functools

import jax
import jax.numpy as jnp
from jax import lax
from jax.experimental import pallas as pl
from jax.experimental.pallas import tpu as pltpu
from jax.sharding import PartitionSpec as P

MESH = pl.DeviceIdType.MESH
F32 = jnp.float32
BF16 = jnp.bfloat16

DP = 32
SP = 8
CHIPS = 16
C0, C1, C2 = 32, 64, 128
X, Y, Z = 4, 8, 128
R1, R2 = 27, 54
VMEM_BYTES = 48 * 1024 * 1024
FACTOR_ONE = float(1048576) ** (-0.5)
FACTOR_TWO = float(131072) ** (-0.5)


def dot(a, b):
    return lax.dot_general(a, b, (((1,), (0,)), ((), ())), preferred_element_type=F32)


def dot_nt(a, b):
    return lax.dot_general(a, b, (((1,), (1,)), ((), ())), preferred_element_type=F32)


def lanes(rows):
    return lax.broadcasted_iota(jnp.int32, (rows, Z), 1)


def shifted(tile, by):
    moved = pltpu.roll(tile, by % Z, 1)
    at = lanes(tile.shape[0])
    keep = at >= by if by > 0 else at < Z + by
    return jnp.where(keep, moved, 0.0)


def frame_plane(source, dest, rows, count, step):
    zero = jnp.zeros((3 * rows, Z), BF16)
    dest[0 : 3 * rows, 0:Z] = zero
    dest[6 * rows : 9 * rows, (count - 1) * Z : count * Z] = zero
    for y in range(count):
        wide = source(y)
        three = [t.astype(BF16) for t in (shifted(wide, step), wide, shifted(wide, -step))]
        for b in range(3):
            to = y - b + 1
            if 0 <= to < count:
                for c in range(3):
                    row = (b * 3 + c) * rows
                    dest[row : row + rows, to * Z : (to + 1) * Z] = three[c]


def gather_taps(parts, rows, count, y, step):
    total = None
    for c in range(3):
        column = None
        for b in range(3):
            at = y - b + 1
            if 0 <= at < count:
                row = (b * 3 + c) * rows
                piece = parts[row : row + rows, at * Z : (at + 1) * Z]
                column = piece if column is None else column + piece
        if c == 0:
            column = shifted(column, -step)
        elif c == 2:
            column = shifted(column, step)
        total = column if total is None else total + column
    return total


def kernel(
    vol_in, wone_in, wtwo_in, cot_in,
    pooled_out, vgrad_out, gone_out, gtwo_out,
    vol, wone, wtwo, cot, vh, fst, s1, pre1, slope1, pp, ps, ph, s2, pre2, d2, es, eh, d1, taps1, grow, taps2, edge2, fs, fh,
    wpad, wsend, wg1, wg2, wf1, wf2, w1, w2, w1t, w2t,
    gs1, gs2, gp1, gp2, ra1, ra2, pb1, pb2, rb1, rb2, sc1, sc2, rc1, rc2,
    in_sem, halo_send, halo_recv, pair_send, pair_recv,
    w1_send, w1_recv, w2_send, w2_recv,
    b1_send, b1_recv, b2_send, b2_recv, c1_send, c1_recv, c2_send, c2_recv,
):
    d = lax.axis_index("dp")
    s = lax.axis_index("space")
    core = lax.rem(d, 2)
    chip = d // 2
    sibling = chip * 2 + 1 - core

    def remote(src, dst, ssem, rsem, **where):
        return pltpu.make_async_remote_copy(
            src_ref=src, dst_ref=dst, send_sem=ssem, recv_sem=rsem,
            device_id=where, device_id_type=MESH,
        )

    def whole(view, ssem, rsem):
        return remote(view, view, ssem, rsem, dp=sibling)

    def each(low, high, action):
        def body(k, carry):
            action(k)
            return carry

        lax.fori_loop(low, high, body, 0)

    def peer(k):
        return lax.rem(chip + k, CHIPS) * 2 + core

    def greet(**where):
        pl.semaphore_signal(barrier, inc=1, device_id=where, device_id_type=MESH)

    barrier = pltpu.get_barrier_semaphore()
    loads = [
        pltpu.make_async_copy(src, dst, in_sem.at[k])
        for k, (src, dst) in enumerate(((wone_in, wone), (wtwo_in, wtwo), (vol_in, vol), (cot_in, cot)))
    ]
    for load in loads:
        load.start()
    each(1, CHIPS, lambda k: greet(dp=peer(k)))
    each(1, SP, lambda k: greet(space=lax.rem(s + k, SP)))
    greet(dp=sibling)

    loads[0].wait()
    loads[1].wait()
    wpad[0:R1] = wone[...].astype(F32)
    wpad[R1:32] = jnp.zeros((32 - R1, C1), F32)
    wsend[0:16] = jnp.concatenate([wpad[0:16], wpad[16:32]], axis=1).astype(BF16)
    wsend[16 : 16 + R2] = wtwo[...]
    wsend[16 + R2 : 80] = jnp.zeros((64 - R2, C2), BF16)
    wg1[chip, core] = wsend[0:16]
    wg2[chip, core] = wsend[16:80]
    loads[2].wait()
    for k in range(2):
        vh[k] = vol[0, :, 0 if k == 0 else X - 1]
    pl.semaphore_wait(barrier, CHIPS - 1 + SP - 1 + 1)

    def halo(n, low_src, high_src, low_dst, high_dst):
        up = remote(high_src, low_dst, halo_send.at[n, 0], halo_recv.at[n, 0], space=lax.rem(s + 1, SP))
        down = remote(low_src, high_dst, halo_send.at[n, 1], halo_recv.at[n, 1], space=lax.rem(s + SP - 1, SP))

        def start():
            @pl.when(s < SP - 1)
            def _():
                up.start()

            @pl.when(s > 0)
            def _():
                down.start()

        def wait():
            @pl.when(s > 0)
            def _():
                up.wait_recv()

            @pl.when(s == 0)
            def _():
                low_dst[...] = jnp.zeros(low_dst.shape, BF16)

            @pl.when(s < SP - 1)
            def _():
                down.wait_recv()

            @pl.when(s == SP - 1)
            def _():
                high_dst[...] = jnp.zeros(high_dst.shape, BF16)

        def drain():
            @pl.when(s < SP - 1)
            def _():
                up.wait_send()

            @pl.when(s > 0)
            def _():
                down.wait_send()

        return start, wait, drain

    def w1_copy(k):
        return remote(wsend.at[pl.ds(0, 16)], wg1.at[chip, core], w1_send, w1_recv, dp=peer(k))

    def w2_copy(k):
        return remote(wsend.at[pl.ds(16, 64)], wg2.at[chip, core], w2_send, w2_recv, dp=peer(k))

    w1_all = whole(wg1.at[pl.ds(1, CHIPS - 1), 0], w1_send, w1_recv)
    w2_all = whole(wg2.at[pl.ds(1, CHIPS - 1), 0], w2_send, w2_recv)
    b1_all = whole(rb1.at[pl.ds(1, CHIPS - 1)], b1_send, b1_recv)
    b2_all = whole(rb2.at[pl.ds(1, CHIPS - 1)], b2_send, b2_recv)
    c1_all = whole(rc1.at[pl.ds(1, SP - 1)], c1_send, c1_recv)
    c2_all = whole(rc2.at[pl.ds(1, SP - 1)], c2_send, c2_recv)
    each(1, CHIPS, lambda k: w1_copy(k).start())
    v_start, v_wait, v_drain = halo(0, vh.at[0], vh.at[1], vh.at[2], vh.at[3])
    v_start()
    each(1, CHIPS, lambda k: w2_copy(k).start())

    def frame_input(plane, dest):
        fst[...] = plane.astype(F32).reshape(C0 * Y, Z)
        frame_plane(lambda y: fst[pl.ds(y, C0, stride=Y), :], dest, C0, Y, 1)

    each(0, X, lambda k: frame_input(vol[0, :, k], s1.at[k + 1]))

    w1_all.wait_recv()
    forward1 = remote(wg1.at[:, core], wg1.at[:, core], pair_send.at[0], pair_recv.at[0], dp=sibling)
    forward1.start()
    v_wait()
    each(0, 2, lambda k: frame_input(vh[k + 2], s1.at[k * (X + 1)]))
    forward1.wait_recv()
    for k in range(DP):
        block = wg1[k // 2, k % 2].astype(F32)
        wf1[R1 * k : R1 * k + 16, 0:C1] = block[:, 0:C1]
        wf1[R1 * k + 16 : R1 * k + R1, 0:C1] = pltpu.roll(block, 64, 1)[0 : R1 - 16, 0:C1]
    w1[...] = wf1[...].astype(BF16)
    w1t[...] = wf1[...].T.astype(BF16)

    even = lax.rem(lanes(C1), 2) == 0

    for x in range(X):
        pre1[x] = dot(w1t[...], s1[x : x + 3].reshape(27 * C0, Y * Z))
    for h in range(2):
        for y in range(Y // 2):
            total = jnp.zeros((C1, Z), F32)
            for k in range(2):
                for j in range(2):
                    at = slice((2 * y + j) * Z, (2 * y + j + 1) * Z)
                    t = pre1[2 * h + k, :, at]
                    sigma = jax.nn.sigmoid(t)
                    total = total + t * sigma
                    slope1[2 * h + k, :, at] = sigma * (1.0 + t * (1.0 - sigma)) * 0.125
            other = jnp.where(even, pltpu.roll(total, Z - 1, 1), pltpu.roll(total, 1, 1))
            pp[h, y] = (total + other) * 0.125

    for h in range(2):
        for y in range(2):
            ps[h, y] = jnp.where(even, pp[h, 2 * y], pp[h, 2 * y + 1]).astype(BF16)
    p_start, p_wait, p_drain = halo(1, ps.at[0], ps.at[1], ph.at[0], ph.at[1])
    p_start()

    def apart(pairs, y):
        wide = pairs[y // 2].astype(F32)
        if y % 2 == 0:
            return jnp.where(even, wide, pltpu.roll(wide, 1, 1))
        return jnp.where(even, pltpu.roll(wide, Z - 1, 1), wide)

    w2_all.wait_recv()
    forward2 = remote(wg2.at[:, core], wg2.at[:, core], pair_send.at[1], pair_recv.at[1], dp=sibling)
    forward2.start()
    for h in range(2):
        frame_plane(lambda y: pp[h, y], s2.at[h + 1], C1, Y // 2, 2)
    forward2.wait_recv()
    for k in range(DP):
        wf2[R2 * k : R2 * k + R2, :] = wg2[k // 2, k % 2].astype(F32)[0:R2]
    w2[...] = wf2[...].astype(BF16)
    w2t[...] = wf2[...].T.astype(BF16)
    p_wait()
    for h in range(2):
        frame_plane(lambda y: apart(ph[h], y), s2.at[3 * h], C1, Y // 2, 2)

    loads[3].wait()
    spread = jnp.where(
        lax.broadcasted_iota(jnp.int32, (32, Z), 1) // 4 == lax.broadcasted_iota(jnp.int32, (32, Z), 0), 1.0, 0.0
    ).astype(BF16)
    squeeze = jnp.where(
        lax.broadcasted_iota(jnp.int32, (32, Z), 1) // 4 == lax.broadcasted_iota(jnp.int32, (32, Z), 0), 0.5, 0.0
    ).astype(BF16)
    for x in range(2):
        pre2[x] = dot(w2t[...], s2[x : x + 3].reshape(27 * C1, Y // 2 * Z))
    sums = []
    for y in range(2):
        spreaded = lax.dot_general(cot[y], spread, (((0,), (0,)), ((), ())), preferred_element_type=F32) * 0.125
        total = jnp.zeros((C2, Z), F32)
        for x in range(2):
            for j in range(2):
                at = slice((2 * y + j) * Z, (2 * y + j + 1) * Z)
                t = pre2[x, :, at]
                sigma = jax.nn.sigmoid(t)
                total = total + t * sigma
                d2[x, :, at] = (spreaded * (sigma * (1.0 + t * (1.0 - sigma)))).astype(BF16)
        sums.append(total)

    for k in range(2):
        edge2[k] = dot(w2[1152 * k : 1152 * k + 576], d2[k])
        for y in range(2):
            a, b = (gather_taps(edge2.at[k], C1, Y // 2, 2 * y + j, 2) for j in range(2))
            es[k, y] = jnp.where(even, a, b).astype(BF16)
    e_start, e_wait, e_drain = halo(2, es.at[0], es.at[1], eh.at[0], eh.at[1])
    e_start()

    for a in range(3):
        gs2[a * 576 : (a + 1) * 576, :] = dot_nt(s2[a], d2[0]) + dot_nt(s2[a + 1], d2[1])
    for k in range(DP):
        gp2[k // 2, k % 2, 0:R2, :] = gs2[R2 * k : R2 * k + R2, :].astype(BF16)
        gp2[k // 2, k % 2, R2:64, :] = jnp.zeros((64 - R2, C2), BF16)
    pair2 = remote(gp2.at[:, 1 - core], ra2, pair_send.at[2], pair_recv.at[2], dp=sibling)
    pair2.start()

    for x in range(2):
        left = jnp.concatenate([w2[(x + 1) * 576 : (x + 2) * 576], w2[x * 576 : (x + 1) * 576]], axis=1)
        taps2[x * 576 : (x + 1) * 576] = dot(left, d2[...].reshape(2 * C2, Y // 2 * Z))

    for y in range(2):
        total = sums[y] * 0.125
        high = total.astype(BF16)
        low = (total - high.astype(F32)).astype(BF16)
        pooled_out[y] = (dot_nt(squeeze, high) + dot_nt(squeeze, low)).astype(BF16)

    pair2.wait_recv()

    def add_pair2(k):
        pb2[k] = (gp2[k, core].astype(F32) + ra2[k].astype(F32)).astype(BF16)

    each(0, CHIPS, add_pair2)

    def b2_copy(k):
        return remote(
            pb2.at[lax.rem(chip + k, CHIPS)], rb2.at[k], b2_send, b2_recv, dp=peer(k)
        )

    each(1, CHIPS, lambda k: b2_copy(k).start())

    e_wait()
    for k in range(2):
        d1[k] = jnp.zeros((C1, Y * Z), BF16)
        d1[X + 2 + k] = jnp.zeros((C1, Y * Z), BF16)
    for x in range(2):
        for y in range(Y // 2):
            grad = gather_taps(taps2.at[x * 576 : (x + 1) * 576], C1, Y // 2, y, 2) + apart(eh[x], y)
            grad = grad.astype(BF16).astype(F32)
            for k in range(2):
                for j in range(2):
                    at = slice((2 * y + j) * Z, (2 * y + j + 1) * Z)
                    d1[2 * x + k + 2, :, at] = (grad * slope1[2 * x + k, :, at]).astype(BF16)

    acc = dot_nt(s1[0], d1[0:3].reshape(3 * C1, Y * Z))
    for k in range(1, X + 2):
        acc = acc + dot_nt(s1[k], d1[k : k + 3].reshape(3 * C1, Y * Z))
    for a in range(3):
        gs1[a * 288 : (a + 1) * 288, :] = acc[:, (2 - a) * C1 : (3 - a) * C1]
    for k in range(DP):
        head = gs1[R1 * k : R1 * k + 16, :].astype(BF16)
        tail = jnp.concatenate(
            [gs1[R1 * k + 16 : R1 * k + R1, :], jnp.zeros((32 - R1, C1), F32)], axis=0
        ).astype(BF16)
        gp1[k // 2, k % 2] = jnp.concatenate([head, tail], axis=1)
    pair1 = remote(gp1.at[:, 1 - core], ra1, pair_send.at[3], pair_recv.at[3], dp=sibling)
    pair1.start()

    for k in range(2):
        taps1[k] = dot(w1[576 * k : 576 * k + 288], d1[2 + (X - 1) * k])
        for y in range(Y):
            fs[k, y] = gather_taps(taps1.at[k], C0, Y, y, 1).astype(BF16)
    f_start, f_wait, f_drain = halo(3, fs.at[0], fs.at[1], fh.at[0], fh.at[1])
    f_start()

    pair1.wait_recv()

    def add_pair1(k):
        pb1[k] = (gp1[k, core].astype(F32) + ra1[k].astype(F32)).astype(BF16)

    each(0, CHIPS, add_pair1)

    def b1_copy(k):
        return remote(
            pb1.at[lax.rem(chip + k, CHIPS)], rb1.at[k], b1_send, b1_recv, dp=peer(k)
        )

    each(1, CHIPS, lambda k: b1_copy(k).start())

    left1 = jnp.concatenate([w1[576:864], w1[288:576], w1[0:288]], axis=1)

    def volume_grad(x, extra=None):
        taps1[x] = dot(left1, d1[x + 1 : x + 4].reshape(3 * C1, Y * Z))
        for y in range(Y):
            piece = gather_taps(taps1.at[x], C0, Y, y, 1)
            if extra is not None:
                piece = piece + extra[y].astype(F32)
            grow[x, pl.ds(y, C0, stride=Y), :] = piece
        vgrad_out[x] = grow[x].reshape(C0, Y, Z).astype(BF16)

    for x in range(1, X - 1):
        volume_grad(x)
    b2_all.wait_recv()
    sum2 = lax.fori_loop(1, CHIPS, lambda k, t: t + rb2[k].astype(F32), pb2[chip].astype(F32))
    sc2[...] = sum2.astype(BF16)

    def c2_copy(k):
        return remote(sc2, rc2.at[k], c2_send, c2_recv, space=lax.rem(s + k, SP))

    each(1, SP, lambda k: c2_copy(k).start())
    f_wait()
    for k in range(2):
        volume_grad((X - 1) * k, fh.at[k])

    b1_all.wait_recv()
    sum1 = lax.fori_loop(1, CHIPS, lambda k, t: t + rb1[k].astype(F32), pb1[chip].astype(F32))
    sc1[...] = sum1.astype(BF16)

    def c1_copy(k):
        return remote(sc1, rc1.at[k], c1_send, c1_recv, space=lax.rem(s + k, SP))

    each(1, SP, lambda k: c1_copy(k).start())
    c2_all.wait_recv()
    full2 = lax.fori_loop(1, SP, lambda k, t: t + rc2[k].astype(F32), sc2[...].astype(F32))
    gtwo_out[...] = full2[0:R2] * (0.5 * FACTOR_TWO)

    v_drain()
    p_drain()
    e_drain()
    f_drain()
    w1_all.wait_send()
    w2_all.wait_send()
    b2_all.wait_send()
    b1_all.wait_send()
    forward1.wait_send()
    forward2.wait_send()
    pair1.wait_send()
    pair2.wait_send()
    c2_all.wait_send()
    c1_all.wait_send()

    c1_all.wait_recv()
    full1 = lax.fori_loop(1, SP, lambda k, t: t + rc1[k].astype(F32), sc1[...].astype(F32))
    gone_out[0:16, :] = full1[:, 0:C1] * FACTOR_ONE
    gone_out[16:R1, :] = pltpu.roll(full1, 64, 1)[0 : R1 - 16, 0:C1] * FACTOR_ONE


def hand_over(pooled, vgrad, gone, gtwo, pooled_to, vgrad_to, gone_to, gtwo_to, sem):
    stores = [pltpu.make_async_copy(vgrad.at[x], vgrad_to.at[0, :, x], sem.at[x]) for x in range(X)]
    stores += [
        pltpu.make_async_copy(src, dst, sem.at[X + k])
        for k, (src, dst) in enumerate(((pooled, pooled_to), (gone, gone_to), (gtwo, gtwo_to)))
    ]
    for store in stores:
        store.start()
    for store in stores:
        store.wait()


def local(volumes, w_first, w_second, cotangent):
    cot = cotangent[0, :, 0].transpose(1, 2, 0)
    hbm = pl.BlockSpec(memory_space=pltpu.HBM)
    shapes = (
        jax.ShapeDtypeStruct((2, 32, C2), BF16),
        jax.ShapeDtypeStruct((1, C0, X, Y, Z), BF16),
        jax.ShapeDtypeStruct((R1, C1), F32),
        jax.ShapeDtypeStruct((R2, C2), F32),
    )
    dma = pltpu.SemaphoreType.DMA
    vmem = pl.BlockSpec(memory_space=pltpu.VMEM)
    results = pl.pallas_call(
        kernel,
        out_shape=(
            pltpu.VMEM((2, 32, C2), BF16),
            pltpu.VMEM((X, C0, Y, Z), BF16),
            pltpu.VMEM((R1, C1), F32),
            pltpu.VMEM((R2, C2), F32),
        ),
        in_specs=[hbm] * 4,
        out_specs=(vmem,) * 4,
        scratch_shapes=[
            pltpu.VMEM((1, C0, X, Y, Z), BF16),
            pltpu.VMEM((R1, C1), BF16),
            pltpu.VMEM((R2, C2), BF16),
            pltpu.VMEM((2, 32, C2), BF16),
            pltpu.VMEM((4, C0, Y, Z), BF16),
            pltpu.VMEM((C0 * Y, Z), F32),
            pltpu.VMEM((X + 2, 9 * C0, Y * Z), BF16),
            pltpu.VMEM((X, C1, Y * Z), F32),
            pltpu.VMEM((X, C1, Y * Z), F32),
            pltpu.VMEM((2, Y // 2, C1, Z), F32),
            pltpu.VMEM((2, 2, C1, Z), BF16),
            pltpu.VMEM((2, 2, C1, Z), BF16),
            pltpu.VMEM((4, 9 * C1, Y // 2 * Z), BF16),
            pltpu.VMEM((2, C2, Y // 2 * Z), F32),
            pltpu.VMEM((2, C2, Y // 2 * Z), BF16),
            pltpu.VMEM((2, 2, C1, Z), BF16),
            pltpu.VMEM((2, 2, C1, Z), BF16),
            pltpu.VMEM((X + 4, C1, Y * Z), BF16),
            pltpu.VMEM((X, 9 * C0, Y * Z), F32),
            pltpu.VMEM((X, C0 * Y, Z), F32),
            pltpu.VMEM((18 * C1, Y // 2 * Z), F32),
            pltpu.VMEM((2, 9 * C1, Y // 2 * Z), F32),
            pltpu.VMEM((2, Y, C0, Z), BF16),
            pltpu.VMEM((2, Y, C0, Z), BF16),
            pltpu.VMEM((32, C1), F32),
            pltpu.VMEM((80, 128), BF16),
            pltpu.VMEM((CHIPS, 2, 16, 128), BF16),
            pltpu.VMEM((CHIPS, 2, 64, 128), BF16),
            pltpu.VMEM((27 * C0, C1), F32),
            pltpu.VMEM((27 * C1, C2), F32),
            pltpu.VMEM((27 * C0, C1), BF16),
            pltpu.VMEM((27 * C1, C2), BF16),
            pltpu.VMEM((C1, 27 * C0), BF16),
            pltpu.VMEM((C2, 27 * C1), BF16),
            pltpu.VMEM((27 * C0, C1), F32),
            pltpu.VMEM((27 * C1, C2), F32),
            pltpu.VMEM((CHIPS, 2, 16, 128), BF16),
            pltpu.VMEM((CHIPS, 2, 64, 128), BF16),
            pltpu.VMEM((CHIPS, 16, 128), BF16),
            pltpu.VMEM((CHIPS, 64, 128), BF16),
            pltpu.VMEM((CHIPS, 16, 128), BF16),
            pltpu.VMEM((CHIPS, 64, 128), BF16),
            pltpu.VMEM((CHIPS, 16, 128), BF16),
            pltpu.VMEM((CHIPS, 64, 128), BF16),
            pltpu.VMEM((16, 128), BF16),
            pltpu.VMEM((64, 128), BF16),
            pltpu.VMEM((SP, 16, 128), BF16),
            pltpu.VMEM((SP, 64, 128), BF16),
            dma((4,)),
            dma((4, 2)), dma((4, 2)),
            dma((4,)), dma((4,)),
            dma, dma,
            dma, dma,
            dma, dma,
            dma, dma,
            dma, dma,
            dma, dma,
        ],
        compiler_params=pltpu.CompilerParams(
            collective_id=0, has_side_effects=True, vmem_limit_bytes=VMEM_BYTES
        ),
    )(*(pltpu.with_memory_space_constraint(each, pltpu.HBM) for each in (volumes, w_first, w_second, cot)))
    pooled, vgrad, gone, gtwo = pl.pallas_call(
        hand_over,
        out_shape=shapes,
        in_specs=[vmem] * 4,
        out_specs=(hbm,) * 4,
        scratch_shapes=[dma((X + 3,))],
        compiler_params=pltpu.CompilerParams(vmem_limit_bytes=VMEM_BYTES),
    )(*results)
    return (pooled.transpose(2, 0, 1)[None, :, None], vgrad, gone, gtwo)


def solution(mesh):
    return jax.shard_map(
        local,
        mesh=mesh,
        in_specs=(
            P("dp", None, "space", None, None),
            P("dp", None),
            P("dp", None),
            P("dp", None, "space", None, None),
        ),
        out_specs=(
            P("dp", None, "space", None, None),
            P("dp", None, "space", None, None),
            P("dp", None),
            P("dp", None),
        ),
        check_vma=False,
    )
```

```python
import functools

import jax
import jax.numpy as jnp
from jax import lax
from jax.experimental import pallas as pl
from jax.experimental.pallas import tpu as pltpu
from jax.sharding import PartitionSpec as P

MESH = pl.DeviceIdType.MESH
F32 = jnp.float32
BF16 = jnp.bfloat16

DP = 32
SP = 8
CHIPS = 16
C0, C1, C2 = 32, 64, 128
X, Y, Z = 4, 8, 128
R1, R2 = 27, 54
VMEM_BYTES = 48 * 1024 * 1024
FACTOR_ONE = float(1048576) ** (-0.5)
FACTOR_TWO = float(131072) ** (-0.5)


def dot(a, b):
    return lax.dot_general(a, b, (((1,), (0,)), ((), ())), preferred_element_type=F32)


def dot_nt(a, b):
    return lax.dot_general(a, b, (((1,), (1,)), ((), ())), preferred_element_type=F32)


def lanes(rows):
    return lax.broadcasted_iota(jnp.int32, (rows, Z), 1)


def shifted(tile, by):
    moved = pltpu.roll(tile, by % Z, 1)
    at = lanes(tile.shape[0])
    keep = at >= by if by > 0 else at < Z + by
    return jnp.where(keep, moved, 0.0)


def frame_plane(source, dest, rows, count, step):
    zero = jnp.zeros((3 * rows, Z), BF16)
    dest[0 : 3 * rows, 0:Z] = zero
    dest[6 * rows : 9 * rows, (count - 1) * Z : count * Z] = zero
    for y in range(count):
        wide = source(y)
        three = [t.astype(BF16) for t in (shifted(wide, step), wide, shifted(wide, -step))]
        for b in range(3):
            to = y - b + 1
            if 0 <= to < count:
                for c in range(3):
                    row = (b * 3 + c) * rows
                    dest[row : row + rows, to * Z : (to + 1) * Z] = three[c]


def gather_taps(parts, rows, count, y, step):
    total = None
    for c in range(3):
        column = None
        for b in range(3):
            at = y - b + 1
            if 0 <= at < count:
                row = (b * 3 + c) * rows
                piece = parts[row : row + rows, at * Z : (at + 1) * Z]
                column = piece if column is None else column + piece
        if c == 0:
            column = shifted(column, -step)
        elif c == 2:
            column = shifted(column, step)
        total = column if total is None else total + column
    return total


def kernel(
    vol_in, wone_in, wtwo_in, cot_in,
    pooled_out, vgrad_out, gone_out, gtwo_out,
    vol, wone, wtwo, cot, vh, fst, s1, pre1, slope1, pp, ps, ph, s2, pre2, d2, es, eh, d1, taps1, grow, taps2, edge2, fs, fh,
    wpad, wsend, wg1, wg2, wf1, wf2, w1, w2, w1t, w2t,
    gs1, gs2, gp1, gp2, ra1, ra2, pb1, pb2, rb1, rb2, sc1, sc2, rc1, rc2,
    in_sem, halo_send, halo_recv, pair_send, pair_recv,
    w1_send, w1_recv, w2_send, w2_recv,
    b1_send, b1_recv, b2_send, b2_recv, c1_send, c1_recv, c2_send, c2_recv,
):
    d = lax.axis_index("dp")
    s = lax.axis_index("space")
    core = lax.rem(d, 2)
    chip = d // 2
    sibling = chip * 2 + 1 - core

    def remote(src, dst, ssem, rsem, **where):
        return pltpu.make_async_remote_copy(
            src_ref=src, dst_ref=dst, send_sem=ssem, recv_sem=rsem,
            device_id=where, device_id_type=MESH,
        )

    def whole(view, ssem, rsem):
        return remote(view, view, ssem, rsem, dp=sibling)

    def each(low, high, action):
        def body(k, carry):
            action(k)
            return carry

        lax.fori_loop(low, high, body, 0)

    def peer(k):
        return lax.rem(chip + k, CHIPS) * 2 + core

    def greet(**where):
        pl.semaphore_signal(barrier, inc=1, device_id=where, device_id_type=MESH)

    barrier = pltpu.get_barrier_semaphore()
    loads = [
        pltpu.make_async_copy(src, dst, in_sem.at[k])
        for k, (src, dst) in enumerate(((wone_in, wone), (wtwo_in, wtwo), (vol_in, vol), (cot_in, cot)))
    ]
    for load in loads:
        load.start()
    each(1, CHIPS, lambda k: greet(dp=peer(k)))
    each(1, SP, lambda k: greet(space=lax.rem(s + k, SP)))
    greet(dp=sibling)

    loads[0].wait()
    loads[1].wait()
    wpad[0:R1] = wone[...].astype(F32)
    wpad[R1:32] = jnp.zeros((32 - R1, C1), F32)
    wsend[0:16] = jnp.concatenate([wpad[0:16], wpad[16:32]], axis=1).astype(BF16)
    wsend[16 : 16 + R2] = wtwo[...]
    wsend[16 + R2 : 80] = jnp.zeros((64 - R2, C2), BF16)
    wg1[chip, core] = wsend[0:16]
    wg2[chip, core] = wsend[16:80]
    loads[2].wait()
    for k in range(2):
        vh[k] = vol[0, :, 0 if k == 0 else X - 1]
    pl.semaphore_wait(barrier, CHIPS - 1 + SP - 1 + 1)

    def halo(n, low_src, high_src, low_dst, high_dst):
        up = remote(high_src, low_dst, halo_send.at[n, 0], halo_recv.at[n, 0], space=lax.rem(s + 1, SP))
        down = remote(low_src, high_dst, halo_send.at[n, 1], halo_recv.at[n, 1], space=lax.rem(s + SP - 1, SP))

        def start():
            @pl.when(s < SP - 1)
            def _():
                up.start()

            @pl.when(s > 0)
            def _():
                down.start()

        def wait():
            @pl.when(s > 0)
            def _():
                up.wait_recv()

            @pl.when(s == 0)
            def _():
                low_dst[...] = jnp.zeros(low_dst.shape, BF16)

            @pl.when(s < SP - 1)
            def _():
                down.wait_recv()

            @pl.when(s == SP - 1)
            def _():
                high_dst[...] = jnp.zeros(high_dst.shape, BF16)

        def drain():
            @pl.when(s < SP - 1)
            def _():
                up.wait_send()

            @pl.when(s > 0)
            def _():
                down.wait_send()

        return start, wait, drain

    def w1_copy(k):
        return remote(wsend.at[pl.ds(0, 16)], wg1.at[chip, core], w1_send, w1_recv, dp=peer(k))

    def w2_copy(k):
        return remote(wsend.at[pl.ds(16, 64)], wg2.at[chip, core], w2_send, w2_recv, dp=peer(k))

    w1_all = whole(wg1.at[pl.ds(1, CHIPS - 1), 0], w1_send, w1_recv)
    w2_all = whole(wg2.at[pl.ds(1, CHIPS - 1), 0], w2_send, w2_recv)
    b1_all = whole(rb1.at[pl.ds(1, CHIPS - 1)], b1_send, b1_recv)
    b2_all = whole(rb2.at[pl.ds(1, CHIPS - 1)], b2_send, b2_recv)
    c1_all = whole(rc1.at[pl.ds(1, SP - 1)], c1_send, c1_recv)
    c2_all = whole(rc2.at[pl.ds(1, SP - 1)], c2_send, c2_recv)
    each(1, CHIPS, lambda k: w1_copy(k).start())
    v_start, v_wait, v_drain = halo(0, vh.at[0], vh.at[1], vh.at[2], vh.at[3])
    v_start()
    each(1, CHIPS, lambda k: w2_copy(k).start())

    def frame_input(plane, dest):
        fst[...] = plane.astype(F32).reshape(C0 * Y, Z)
        frame_plane(lambda y: fst[pl.ds(y, C0, stride=Y), :], dest, C0, Y, 1)

    each(0, X, lambda k: frame_input(vol[0, :, k], s1.at[k + 1]))

    w1_all.wait_recv()
    forward1 = remote(wg1.at[:, core], wg1.at[:, core], pair_send.at[0], pair_recv.at[0], dp=sibling)
    forward1.start()
    v_wait()
    each(0, 2, lambda k: frame_input(vh[k + 2], s1.at[k * (X + 1)]))
    forward1.wait_recv()
    for k in range(DP):
        block = wg1[k // 2, k % 2].astype(F32)
        wf1[R1 * k : R1 * k + 16, 0:C1] = block[:, 0:C1]
        wf1[R1 * k + 16 : R1 * k + R1, 0:C1] = pltpu.roll(block, 64, 1)[0 : R1 - 16, 0:C1]
    w1[...] = wf1[...].astype(BF16)
    w1t[...] = wf1[...].T.astype(BF16)

    even = lax.rem(lanes(C1), 2) == 0

    for x in range(X):
        pre1[x] = dot(w1t[...], s1[x : x + 3].reshape(27 * C0, Y * Z))
    for h in range(2):
        for y in range(Y // 2):
            total = jnp.zeros((C1, Z), F32)
            for k in range(2):
                for j in range(2):
                    at = slice((2 * y + j) * Z, (2 * y + j + 1) * Z)
                    t = pre1[2 * h + k, :, at]
                    sigma = jax.nn.sigmoid(t)
                    total = total + t * sigma
                    slope1[2 * h + k, :, at] = sigma * (1.0 + t * (1.0 - sigma)) * 0.125
            other = jnp.where(even, pltpu.roll(total, Z - 1, 1), pltpu.roll(total, 1, 1))
            pp[h, y] = (total + other) * 0.125

    for h in range(2):
        for y in range(2):
            ps[h, y] = jnp.where(even, pp[h, 2 * y], pp[h, 2 * y + 1]).astype(BF16)
    p_start, p_wait, p_drain = halo(1, ps.at[0], ps.at[1], ph.at[0], ph.at[1])
    p_start()

    def apart(pairs, y):
        wide = pairs[y // 2].astype(F32)
        if y % 2 == 0:
            return jnp.where(even, wide, pltpu.roll(wide, 1, 1))
        return jnp.where(even, pltpu.roll(wide, Z - 1, 1), wide)

    w2_all.wait_recv()
    forward2 = remote(wg2.at[:, core], wg2.at[:, core], pair_send.at[1], pair_recv.at[1], dp=sibling)
    forward2.start()
    for h in range(2):
        frame_plane(lambda y: pp[h, y], s2.at[h + 1], C1, Y // 2, 2)
    forward2.wait_recv()
    for k in range(DP):
        wf2[R2 * k : R2 * k + R2, :] = wg2[k // 2, k % 2].astype(F32)[0:R2]
    w2[...] = wf2[...].astype(BF16)
    w2t[...] = wf2[...].T.astype(BF16)
    p_wait()
    for h in range(2):
        frame_plane(lambda y: apart(ph[h], y), s2.at[3 * h], C1, Y // 2, 2)

    loads[3].wait()
    spread = jnp.where(
        lax.broadcasted_iota(jnp.int32, (32, Z), 1) // 4 == lax.broadcasted_iota(jnp.int32, (32, Z), 0), 1.0, 0.0
    ).astype(BF16)
    squeeze = jnp.where(
        lax.broadcasted_iota(jnp.int32, (32, Z), 1) // 4 == lax.broadcasted_iota(jnp.int32, (32, Z), 0), 0.5, 0.0
    ).astype(BF16)
    for x in range(2):
        pre2[x] = dot(w2t[...], s2[x : x + 3].reshape(27 * C1, Y // 2 * Z))
    sums = []
    for y in range(2):
        spreaded = lax.dot_general(cot[y], spread, (((0,), (0,)), ((), ())), preferred_element_type=F32) * 0.125
        total = jnp.zeros((C2, Z), F32)
        for x in range(2):
            for j in range(2):
                at = slice((2 * y + j) * Z, (2 * y + j + 1) * Z)
                t = pre2[x, :, at]
                sigma = jax.nn.sigmoid(t)
                total = total + t * sigma
                d2[x, :, at] = (spreaded * (sigma * (1.0 + t * (1.0 - sigma)))).astype(BF16)
        sums.append(total)

    for k in range(2):
        edge2[k] = dot(w2[1152 * k : 1152 * k + 576], d2[k])
        for y in range(2):
            a, b = (gather_taps(edge2.at[k], C1, Y // 2, 2 * y + j, 2) for j in range(2))
            es[k, y] = jnp.where(even, a, b).astype(BF16)
    e_start, e_wait, e_drain = halo(2, es.at[0], es.at[1], eh.at[0], eh.at[1])
    e_start()

    parts = [dot_nt(s2[k], d2[...].reshape(2 * C2, Y // 2 * Z)) for k in range(4)]
    for a in range(3):
        gs2[a * 576 : (a + 1) * 576, :] = parts[a][:, 0:128] + parts[a + 1][:, 128:256]
    for k in range(DP):
        gp2[k // 2, k % 2, 0:R2, :] = gs2[R2 * k : R2 * k + R2, :].astype(BF16)
        gp2[k // 2, k % 2, R2:64, :] = jnp.zeros((64 - R2, C2), BF16)
    pair2 = remote(gp2.at[:, 1 - core], ra2, pair_send.at[2], pair_recv.at[2], dp=sibling)
    pair2.start()

    for x in range(2):
        left = jnp.concatenate([w2[(x + 1) * 576 : (x + 2) * 576], w2[x * 576 : (x + 1) * 576]], axis=1)
        taps2[x * 576 : (x + 1) * 576] = dot(left, d2[...].reshape(2 * C2, Y // 2 * Z))

    for y in range(2):
        total = sums[y] * 0.125
        high = total.astype(BF16)
        low = (total - high.astype(F32)).astype(BF16)
        pooled_out[y] = (dot_nt(squeeze, high) + dot_nt(squeeze, low)).astype(BF16)

    pair2.wait_recv()

    def add_pair2(k):
        pb2[k] = (gp2[k, core].astype(F32) + ra2[k].astype(F32)).astype(BF16)

    each(0, CHIPS, add_pair2)

    def b2_copy(k):
        return remote(
            pb2.at[lax.rem(chip + k, CHIPS)], rb2.at[k], b2_send, b2_recv, dp=peer(k)
        )

    each(1, CHIPS, lambda k: b2_copy(k).start())

    e_wait()
    for k in range(2):
        d1[1 + (X + 1) * k] = jnp.zeros((C1, Y * Z), BF16)
    for x in range(2):
        for y in range(Y // 2):
            grad = gather_taps(taps2.at[x * 576 : (x + 1) * 576], C1, Y // 2, y, 2) + apart(eh[x], y)
            grad = grad.astype(BF16).astype(F32)
            for k in range(2):
                for j in range(2):
                    at = slice((2 * y + j) * Z, (2 * y + j + 1) * Z)
                    d1[2 * x + k + 2, :, at] = (grad * slope1[2 * x + k, :, at]).astype(BF16)

    parts = [dot_nt(s1[k], d1[2 : X + 2].reshape(X * C1, Y * Z)) for k in range(X + 2)]
    for a in range(3):
        low = parts[a][:, 0:128] + parts[a + 2][:, 128:256]
        high = parts[a + 1][:, 0:128] + parts[a + 3][:, 128:256]
        gs1[a * 288 : (a + 1) * 288, :] = (low + pltpu.roll(high, 64, 1))[:, 0:C1]
    for k in range(DP):
        head = gs1[R1 * k : R1 * k + 16, :].astype(BF16)
        tail = jnp.concatenate(
            [gs1[R1 * k + 16 : R1 * k + R1, :], jnp.zeros((32 - R1, C1), F32)], axis=0
        ).astype(BF16)
        gp1[k // 2, k % 2] = jnp.concatenate([head, tail], axis=1)
    pair1 = remote(gp1.at[:, 1 - core], ra1, pair_send.at[3], pair_recv.at[3], dp=sibling)
    pair1.start()

    for k in range(2):
        taps1[k] = dot(w1[576 * k : 576 * k + 288], d1[2 + (X - 1) * k])
        for y in range(Y):
            fs[k, y] = gather_taps(taps1.at[k], C0, Y, y, 1).astype(BF16)
    f_start, f_wait, f_drain = halo(3, fs.at[0], fs.at[1], fh.at[0], fh.at[1])
    f_start()

    pair1.wait_recv()

    def add_pair1(k):
        pb1[k] = (gp1[k, core].astype(F32) + ra1[k].astype(F32)).astype(BF16)

    each(0, CHIPS, add_pair1)

    def b1_copy(k):
        return remote(
            pb1.at[lax.rem(chip + k, CHIPS)], rb1.at[k], b1_send, b1_recv, dp=peer(k)
        )

    each(1, CHIPS, lambda k: b1_copy(k).start())

    left1 = jnp.concatenate([w1[576:864], w1[288:576], w1[0:288]], axis=1)

    def volume_grad(x, extra=None):
        taps1[x] = dot(left1, d1[x + 1 : x + 4].reshape(3 * C1, Y * Z))
        for y in range(Y):
            piece = gather_taps(taps1.at[x], C0, Y, y, 1)
            if extra is not None:
                piece = piece + extra[y].astype(F32)
            grow[x, pl.ds(y, C0, stride=Y), :] = piece
        vgrad_out[x] = grow[x].reshape(C0, Y, Z).astype(BF16)

    for x in range(1, X - 1):
        volume_grad(x)
    b2_all.wait_recv()
    sum2 = lax.fori_loop(1, CHIPS, lambda k, t: t + rb2[k].astype(F32), pb2[chip].astype(F32))
    sc2[...] = sum2.astype(BF16)

    def c2_copy(k):
        return remote(sc2, rc2.at[k], c2_send, c2_recv, space=lax.rem(s + k, SP))

    each(1, SP, lambda k: c2_copy(k).start())
    f_wait()
    for k in range(2):
        volume_grad((X - 1) * k, fh.at[k])

    b1_all.wait_recv()
    sum1 = lax.fori_loop(1, CHIPS, lambda k, t: t + rb1[k].astype(F32), pb1[chip].astype(F32))
    sc1[...] = sum1.astype(BF16)

    def c1_copy(k):
        return remote(sc1, rc1.at[k], c1_send, c1_recv, space=lax.rem(s + k, SP))

    each(1, SP, lambda k: c1_copy(k).start())
    c2_all.wait_recv()
    full2 = lax.fori_loop(1, SP, lambda k, t: t + rc2[k].astype(F32), sc2[...].astype(F32))
    gtwo_out[...] = full2[0:R2] * (0.5 * FACTOR_TWO)

    v_drain()
    p_drain()
    e_drain()
    f_drain()
    w1_all.wait_send()
    w2_all.wait_send()
    b2_all.wait_send()
    b1_all.wait_send()
    forward1.wait_send()
    forward2.wait_send()
    pair1.wait_send()
    pair2.wait_send()
    c2_all.wait_send()
    c1_all.wait_send()

    c1_all.wait_recv()
    full1 = lax.fori_loop(1, SP, lambda k, t: t + rc1[k].astype(F32), sc1[...].astype(F32))
    gone_out[0:16, :] = full1[:, 0:C1] * FACTOR_ONE
    gone_out[16:R1, :] = pltpu.roll(full1, 64, 1)[0 : R1 - 16, 0:C1] * FACTOR_ONE


def hand_over(pooled, vgrad, gone, gtwo, pooled_to, vgrad_to, gone_to, gtwo_to, sem):
    stores = [pltpu.make_async_copy(vgrad.at[x], vgrad_to.at[0, :, x], sem.at[x]) for x in range(X)]
    stores += [
        pltpu.make_async_copy(src, dst, sem.at[X + k])
        for k, (src, dst) in enumerate(((pooled, pooled_to), (gone, gone_to), (gtwo, gtwo_to)))
    ]
    for store in stores:
        store.start()
    for store in stores:
        store.wait()


def local(volumes, w_first, w_second, cotangent):
    cot = cotangent[0, :, 0].transpose(1, 2, 0)
    hbm = pl.BlockSpec(memory_space=pltpu.HBM)
    shapes = (
        jax.ShapeDtypeStruct((2, 32, C2), BF16),
        jax.ShapeDtypeStruct((1, C0, X, Y, Z), BF16),
        jax.ShapeDtypeStruct((R1, C1), F32),
        jax.ShapeDtypeStruct((R2, C2), F32),
    )
    dma = pltpu.SemaphoreType.DMA
    vmem = pl.BlockSpec(memory_space=pltpu.VMEM)
    results = pl.pallas_call(
        kernel,
        out_shape=(
            pltpu.VMEM((2, 32, C2), BF16),
            pltpu.VMEM((X, C0, Y, Z), BF16),
            pltpu.VMEM((R1, C1), F32),
            pltpu.VMEM((R2, C2), F32),
        ),
        in_specs=[hbm] * 4,
        out_specs=(vmem,) * 4,
        scratch_shapes=[
            pltpu.VMEM((1, C0, X, Y, Z), BF16),
            pltpu.VMEM((R1, C1), BF16),
            pltpu.VMEM((R2, C2), BF16),
            pltpu.VMEM((2, 32, C2), BF16),
            pltpu.VMEM((4, C0, Y, Z), BF16),
            pltpu.VMEM((C0 * Y, Z), F32),
            pltpu.VMEM((X + 2, 9 * C0, Y * Z), BF16),
            pltpu.VMEM((X, C1, Y * Z), F32),
            pltpu.VMEM((X, C1, Y * Z), F32),
            pltpu.VMEM((2, Y // 2, C1, Z), F32),
            pltpu.VMEM((2, 2, C1, Z), BF16),
            pltpu.VMEM((2, 2, C1, Z), BF16),
            pltpu.VMEM((4, 9 * C1, Y // 2 * Z), BF16),
            pltpu.VMEM((2, C2, Y // 2 * Z), F32),
            pltpu.VMEM((2, C2, Y // 2 * Z), BF16),
            pltpu.VMEM((2, 2, C1, Z), BF16),
            pltpu.VMEM((2, 2, C1, Z), BF16),
            pltpu.VMEM((X + 4, C1, Y * Z), BF16),
            pltpu.VMEM((X, 9 * C0, Y * Z), F32),
            pltpu.VMEM((X, C0 * Y, Z), F32),
            pltpu.VMEM((18 * C1, Y // 2 * Z), F32),
            pltpu.VMEM((2, 9 * C1, Y // 2 * Z), F32),
            pltpu.VMEM((2, Y, C0, Z), BF16),
            pltpu.VMEM((2, Y, C0, Z), BF16),
            pltpu.VMEM((32, C1), F32),
            pltpu.VMEM((80, 128), BF16),
            pltpu.VMEM((CHIPS, 2, 16, 128), BF16),
            pltpu.VMEM((CHIPS, 2, 64, 128), BF16),
            pltpu.VMEM((27 * C0, C1), F32),
            pltpu.VMEM((27 * C1, C2), F32),
            pltpu.VMEM((27 * C0, C1), BF16),
            pltpu.VMEM((27 * C1, C2), BF16),
            pltpu.VMEM((C1, 27 * C0), BF16),
            pltpu.VMEM((C2, 27 * C1), BF16),
            pltpu.VMEM((27 * C0, C1), F32),
            pltpu.VMEM((27 * C1, C2), F32),
            pltpu.VMEM((CHIPS, 2, 16, 128), BF16),
            pltpu.VMEM((CHIPS, 2, 64, 128), BF16),
            pltpu.VMEM((CHIPS, 16, 128), BF16),
            pltpu.VMEM((CHIPS, 64, 128), BF16),
            pltpu.VMEM((CHIPS, 16, 128), BF16),
            pltpu.VMEM((CHIPS, 64, 128), BF16),
            pltpu.VMEM((CHIPS, 16, 128), BF16),
            pltpu.VMEM((CHIPS, 64, 128), BF16),
            pltpu.VMEM((16, 128), BF16),
            pltpu.VMEM((64, 128), BF16),
            pltpu.VMEM((SP, 16, 128), BF16),
            pltpu.VMEM((SP, 64, 128), BF16),
            dma((4,)),
            dma((4, 2)), dma((4, 2)),
            dma((4,)), dma((4,)),
            dma, dma,
            dma, dma,
            dma, dma,
            dma, dma,
            dma, dma,
            dma, dma,
        ],
        compiler_params=pltpu.CompilerParams(
            collective_id=0, has_side_effects=True, vmem_limit_bytes=VMEM_BYTES
        ),
    )(*(pltpu.with_memory_space_constraint(each, pltpu.HBM) for each in (volumes, w_first, w_second, cot)))
    pooled, vgrad, gone, gtwo = pl.pallas_call(
        hand_over,
        out_shape=shapes,
        in_specs=[vmem] * 4,
        out_specs=(hbm,) * 4,
        scratch_shapes=[dma((X + 3,))],
        compiler_params=pltpu.CompilerParams(vmem_limit_bytes=VMEM_BYTES),
    )(*results)
    return (pooled.transpose(2, 0, 1)[None, :, None], vgrad, gone, gtwo)


def solution(mesh):
    return jax.shard_map(
        local,
        mesh=mesh,
        in_specs=(
            P("dp", None, "space", None, None),
            P("dp", None),
            P("dp", None),
            P("dp", None, "space", None, None),
        ),
        out_specs=(
            P("dp", None, "space", None, None),
            P("dp", None, "space", None, None),
            P("dp", None),
            P("dp", None),
        ),
        check_vma=False,
    )
```

```python
import functools

import jax
import jax.numpy as jnp
from jax import lax
from jax.experimental import pallas as pl
from jax.experimental.pallas import tpu as pltpu
from jax.sharding import PartitionSpec as P

MESH = pl.DeviceIdType.MESH
F32 = jnp.float32
BF16 = jnp.bfloat16

DP = 32
SP = 8
CHIPS = 16
C0, C1, C2 = 32, 64, 128
X, Y, Z = 4, 8, 128
R1, R2 = 27, 54
VMEM_BYTES = 48 * 1024 * 1024
FAR_CHIPS = (12, 11, 13, 4, 10, 14, 3, 5, 9, 15, 2, 6, 8, 1, 7)
FACTOR_ONE = float(1048576) ** (-0.5)
FACTOR_TWO = float(131072) ** (-0.5)


def dot(a, b):
    return lax.dot_general(a, b, (((1,), (0,)), ((), ())), preferred_element_type=F32)


def dot_nt(a, b):
    return lax.dot_general(a, b, (((1,), (1,)), ((), ())), preferred_element_type=F32)


def lanes(rows):
    return lax.broadcasted_iota(jnp.int32, (rows, Z), 1)


def shifted(tile, by):
    moved = pltpu.roll(tile, by % Z, 1)
    at = lanes(tile.shape[0])
    keep = at >= by if by > 0 else at < Z + by
    return jnp.where(keep, moved, 0.0)


def frame_plane(source, dest, rows, count, step):
    zero = jnp.zeros((3 * rows, Z), BF16)
    dest[0 : 3 * rows, 0:Z] = zero
    dest[6 * rows : 9 * rows, (count - 1) * Z : count * Z] = zero
    for y in range(count):
        wide = source(y)
        three = [t.astype(BF16) for t in (shifted(wide, step), wide, shifted(wide, -step))]
        for b in range(3):
            to = y - b + 1
            if 0 <= to < count:
                for c in range(3):
                    row = (b * 3 + c) * rows
                    dest[row : row + rows, to * Z : (to + 1) * Z] = three[c]


def gather_taps(parts, rows, count, y, step):
    total = None
    for c in range(3):
        column = None
        for b in range(3):
            at = y - b + 1
            if 0 <= at < count:
                row = (b * 3 + c) * rows
                piece = parts[row : row + rows, at * Z : (at + 1) * Z]
                column = piece if column is None else column + piece
        if c == 0:
            column = shifted(column, -step)
        elif c == 2:
            column = shifted(column, step)
        total = column if total is None else total + column
    return total


def kernel(
    vol_in, wone_in, wtwo_in, cot_in,
    pooled_out, vgrad_out, gone_out, gtwo_out,
    vol, wone, wtwo, cot, vh, fst, s1, pre1, slope1, pp, ps, ph, s2, pre2, d2, es, eh, d1, taps1, grow, taps2, edge2, fs, fh,
    wpad, wsend, wg1, wg2, wf1, wf2, w1, w2, w1t, w2t,
    gs1, gs2, gp1, gp2, ra1, ra2, pb1, pb2, rb1, rb2, sc1, sc2, rc1, rc2,
    in_sem, halo_send, halo_recv, pair_send, pair_recv,
    w1_send, w1_recv, w2_send, w2_recv,
    b1_send, b1_recv, b2_send, b2_recv, c1_send, c1_recv, c2_send, c2_recv,
):
    d = lax.axis_index("dp")
    s = lax.axis_index("space")
    core = lax.rem(d, 2)
    chip = d // 2
    sibling = chip * 2 + 1 - core

    def remote(src, dst, ssem, rsem, **where):
        return pltpu.make_async_remote_copy(
            src_ref=src, dst_ref=dst, send_sem=ssem, recv_sem=rsem,
            device_id=where, device_id_type=MESH,
        )

    def whole(view, ssem, rsem):
        return remote(view, view, ssem, rsem, dp=sibling)

    def each(low, high, action):
        def body(k, carry):
            action(k)
            return carry

        lax.fori_loop(low, high, body, 0)

    def peer(k):
        return lax.rem(chip + k, CHIPS) * 2 + core

    def greet(**where):
        pl.semaphore_signal(barrier, inc=1, device_id=where, device_id_type=MESH)

    barrier = pltpu.get_barrier_semaphore()
    loads = [
        pltpu.make_async_copy(src, dst, in_sem.at[k])
        for k, (src, dst) in enumerate(((wone_in, wone), (wtwo_in, wtwo), (vol_in, vol), (cot_in, cot)))
    ]
    for load in loads:
        load.start()
    each(1, CHIPS, lambda k: greet(dp=peer(k)))
    each(1, SP, lambda k: greet(space=lax.rem(s + k, SP)))
    greet(dp=sibling)

    loads[0].wait()
    loads[1].wait()
    wpad[0:R1] = wone[...].astype(F32)
    wpad[R1:32] = jnp.zeros((32 - R1, C1), F32)
    wsend[0:16] = jnp.concatenate([wpad[0:16], wpad[16:32]], axis=1).astype(BF16)
    wsend[16 : 16 + R2] = wtwo[...]
    wsend[16 + R2 : 80] = jnp.zeros((64 - R2, C2), BF16)
    wg1[chip, core] = wsend[0:16]
    wg2[chip, core] = wsend[16:80]
    loads[2].wait()
    for k in range(2):
        vh[k] = vol[0, :, 0 if k == 0 else X - 1]
    pl.semaphore_wait(barrier, CHIPS - 1 + SP - 1 + 1)

    def halo(n, low_src, high_src, low_dst, high_dst):
        up = remote(high_src, low_dst, halo_send.at[n, 0], halo_recv.at[n, 0], space=lax.rem(s + 1, SP))
        down = remote(low_src, high_dst, halo_send.at[n, 1], halo_recv.at[n, 1], space=lax.rem(s + SP - 1, SP))

        def start():
            @pl.when(s < SP - 1)
            def _():
                up.start()

            @pl.when(s > 0)
            def _():
                down.start()

        def wait():
            @pl.when(s > 0)
            def _():
                up.wait_recv()

            @pl.when(s == 0)
            def _():
                low_dst[...] = jnp.zeros(low_dst.shape, BF16)

            @pl.when(s < SP - 1)
            def _():
                down.wait_recv()

            @pl.when(s == SP - 1)
            def _():
                high_dst[...] = jnp.zeros(high_dst.shape, BF16)

        def drain():
            @pl.when(s < SP - 1)
            def _():
                up.wait_send()

            @pl.when(s > 0)
            def _():
                down.wait_send()

        return start, wait, drain

    def w1_copy(k):
        return remote(wsend.at[pl.ds(0, 16)], wg1.at[chip, core], w1_send, w1_recv, dp=peer(k))

    def w2_copy(k):
        return remote(wsend.at[pl.ds(16, 64)], wg2.at[chip, core], w2_send, w2_recv, dp=peer(k))

    w1_all = whole(wg1.at[pl.ds(1, CHIPS - 1), 0], w1_send, w1_recv)
    w2_all = whole(wg2.at[pl.ds(1, CHIPS - 1), 0], w2_send, w2_recv)
    b1_all = whole(rb1.at[pl.ds(1, CHIPS - 1)], b1_send, b1_recv)
    b2_all = whole(rb2.at[pl.ds(1, CHIPS - 1)], b2_send, b2_recv)
    c1_all = whole(rc1.at[pl.ds(1, SP - 1)], c1_send, c1_recv)
    c2_all = whole(rc2.at[pl.ds(1, SP - 1)], c2_send, c2_recv)
    for k in FAR_CHIPS:
        w1_copy(k).start()
    v_start, v_wait, v_drain = halo(0, vh.at[0], vh.at[1], vh.at[2], vh.at[3])
    v_start()
    for k in FAR_CHIPS:
        w2_copy(k).start()

    def frame_input(plane, dest):
        fst[...] = plane.astype(F32).reshape(C0 * Y, Z)
        frame_plane(lambda y: fst[pl.ds(y, C0, stride=Y), :], dest, C0, Y, 1)

    each(0, X, lambda k: frame_input(vol[0, :, k], s1.at[k + 1]))

    w1_all.wait_recv()
    forward1 = remote(wg1.at[:, core], wg1.at[:, core], pair_send.at[0], pair_recv.at[0], dp=sibling)
    forward1.start()
    v_wait()
    each(0, 2, lambda k: frame_input(vh[k + 2], s1.at[k * (X + 1)]))
    forward1.wait_recv()
    for k in range(DP):
        block = wg1[k // 2, k % 2].astype(F32)
        wf1[R1 * k : R1 * k + 16, 0:C1] = block[:, 0:C1]
        wf1[R1 * k + 16 : R1 * k + R1, 0:C1] = pltpu.roll(block, 64, 1)[0 : R1 - 16, 0:C1]
    w1[...] = wf1[...].astype(BF16)
    w1t[...] = wf1[...].T.astype(BF16)

    even = lax.rem(lanes(C1), 2) == 0

    for x in range(X):
        pre1[x] = dot(w1t[...], s1[x : x + 3].reshape(27 * C0, Y * Z))
    for h in range(2):
        for y in range(Y // 2):
            total = jnp.zeros((C1, Z), F32)
            for k in range(2):
                for j in range(2):
                    at = slice((2 * y + j) * Z, (2 * y + j + 1) * Z)
                    t = pre1[2 * h + k, :, at]
                    sigma = jax.nn.sigmoid(t)
                    total = total + t * sigma
                    slope1[2 * h + k, :, at] = sigma * (1.0 + t * (1.0 - sigma)) * 0.125
            other = jnp.where(even, pltpu.roll(total, Z - 1, 1), pltpu.roll(total, 1, 1))
            pp[h, y] = (total + other) * 0.125

    for h in range(2):
        for y in range(2):
            ps[h, y] = jnp.where(even, pp[h, 2 * y], pp[h, 2 * y + 1]).astype(BF16)
    p_start, p_wait, p_drain = halo(1, ps.at[0], ps.at[1], ph.at[0], ph.at[1])
    p_start()

    def apart(pairs, y):
        wide = pairs[y // 2].astype(F32)
        if y % 2 == 0:
            return jnp.where(even, wide, pltpu.roll(wide, 1, 1))
        return jnp.where(even, pltpu.roll(wide, Z - 1, 1), wide)

    w2_all.wait_recv()
    forward2 = remote(wg2.at[:, core], wg2.at[:, core], pair_send.at[1], pair_recv.at[1], dp=sibling)
    forward2.start()
    for h in range(2):
        frame_plane(lambda y: pp[h, y], s2.at[h + 1], C1, Y // 2, 2)
    forward2.wait_recv()
    for k in range(DP):
        wf2[R2 * k : R2 * k + R2, :] = wg2[k // 2, k % 2].astype(F32)[0:R2]
    w2[...] = wf2[...].astype(BF16)
    w2t[...] = wf2[...].T.astype(BF16)
    p_wait()
    for h in range(2):
        frame_plane(lambda y: apart(ph[h], y), s2.at[3 * h], C1, Y // 2, 2)

    loads[3].wait()
    spread = jnp.where(
        lax.broadcasted_iota(jnp.int32, (32, Z), 1) // 4 == lax.broadcasted_iota(jnp.int32, (32, Z), 0), 1.0, 0.0
    ).astype(BF16)
    squeeze = jnp.where(
        lax.broadcasted_iota(jnp.int32, (32, Z), 1) // 4 == lax.broadcasted_iota(jnp.int32, (32, Z), 0), 0.5, 0.0
    ).astype(BF16)
    for x in range(2):
        pre2[x] = dot(w2t[...], s2[x : x + 3].reshape(27 * C1, Y // 2 * Z))
    sums = []
    for y in range(2):
        spreaded = lax.dot_general(cot[y], spread, (((0,), (0,)), ((), ())), preferred_element_type=F32) * 0.125
        total = jnp.zeros((C2, Z), F32)
        for x in range(2):
            for j in range(2):
                at = slice((2 * y + j) * Z, (2 * y + j + 1) * Z)
                t = pre2[x, :, at]
                sigma = jax.nn.sigmoid(t)
                total = total + t * sigma
                d2[x, :, at] = (spreaded * (sigma * (1.0 + t * (1.0 - sigma)))).astype(BF16)
        sums.append(total)

    for k in range(2):
        edge2[k] = dot(w2[1152 * k : 1152 * k + 576], d2[k])
        for y in range(2):
            a, b = (gather_taps(edge2.at[k], C1, Y // 2, 2 * y + j, 2) for j in range(2))
            es[k, y] = jnp.where(even, a, b).astype(BF16)
    e_start, e_wait, e_drain = halo(2, es.at[0], es.at[1], eh.at[0], eh.at[1])
    e_start()

    parts = [dot_nt(s2[k], d2[...].reshape(2 * C2, Y // 2 * Z)) for k in range(4)]
    for a in range(3):
        gs2[a * 576 : (a + 1) * 576, :] = parts[a][:, 0:128] + parts[a + 1][:, 128:256]
    for k in range(DP):
        gp2[k // 2, k % 2, 0:R2, :] = gs2[R2 * k : R2 * k + R2, :].astype(BF16)
        gp2[k // 2, k % 2, R2:64, :] = jnp.zeros((64 - R2, C2), BF16)
    pair2 = remote(gp2.at[:, 1 - core], ra2, pair_send.at[2], pair_recv.at[2], dp=sibling)
    pair2.start()

    for x in range(2):
        left = jnp.concatenate([w2[(x + 1) * 576 : (x + 2) * 576], w2[x * 576 : (x + 1) * 576]], axis=1)
        taps2[x * 576 : (x + 1) * 576] = dot(left, d2[...].reshape(2 * C2, Y // 2 * Z))

    for y in range(2):
        total = sums[y] * 0.125
        high = total.astype(BF16)
        low = (total - high.astype(F32)).astype(BF16)
        pooled_out[y] = (dot_nt(squeeze, high) + dot_nt(squeeze, low)).astype(BF16)

    pair2.wait_recv()

    def add_pair2(k):
        pb2[k] = (gp2[k, core].astype(F32) + ra2[k].astype(F32)).astype(BF16)

    each(0, CHIPS, add_pair2)

    def b2_copy(k):
        return remote(
            pb2.at[lax.rem(chip + k, CHIPS)], rb2.at[k], b2_send, b2_recv, dp=peer(k)
        )

    each(1, CHIPS, lambda k: b2_copy(k).start())

    e_wait()
    for k in range(2):
        d1[1 + (X + 1) * k] = jnp.zeros((C1, Y * Z), BF16)
    for x in range(2):
        for y in range(Y // 2):
            grad = gather_taps(taps2.at[x * 576 : (x + 1) * 576], C1, Y // 2, y, 2) + apart(eh[x], y)
            grad = grad.astype(BF16).astype(F32)
            for k in range(2):
                for j in range(2):
                    at = slice((2 * y + j) * Z, (2 * y + j + 1) * Z)
                    d1[2 * x + k + 2, :, at] = (grad * slope1[2 * x + k, :, at]).astype(BF16)

    parts = [dot_nt(s1[k], d1[2 : X + 2].reshape(X * C1, Y * Z)) for k in range(X + 2)]
    for a in range(3):
        low = parts[a][:, 0:128] + parts[a + 2][:, 128:256]
        high = parts[a + 1][:, 0:128] + parts[a + 3][:, 128:256]
        gs1[a * 288 : (a + 1) * 288, :] = (low + pltpu.roll(high, 64, 1))[:, 0:C1]
    for k in range(DP):
        head = gs1[R1 * k : R1 * k + 16, :].astype(BF16)
        tail = jnp.concatenate(
            [gs1[R1 * k + 16 : R1 * k + R1, :], jnp.zeros((32 - R1, C1), F32)], axis=0
        ).astype(BF16)
        gp1[k // 2, k % 2] = jnp.concatenate([head, tail], axis=1)
    pair1 = remote(gp1.at[:, 1 - core], ra1, pair_send.at[3], pair_recv.at[3], dp=sibling)
    pair1.start()

    for k in range(2):
        taps1[k] = dot(w1[576 * k : 576 * k + 288], d1[2 + (X - 1) * k])
        for y in range(Y):
            fs[k, y] = gather_taps(taps1.at[k], C0, Y, y, 1).astype(BF16)
    f_start, f_wait, f_drain = halo(3, fs.at[0], fs.at[1], fh.at[0], fh.at[1])
    f_start()

    pair1.wait_recv()

    def add_pair1(k):
        pb1[k] = (gp1[k, core].astype(F32) + ra1[k].astype(F32)).astype(BF16)

    each(0, CHIPS, add_pair1)

    def b1_copy(k):
        return remote(
            pb1.at[lax.rem(chip + k, CHIPS)], rb1.at[k], b1_send, b1_recv, dp=peer(k)
        )

    each(1, CHIPS, lambda k: b1_copy(k).start())

    left1 = jnp.concatenate([w1[576:864], w1[288:576], w1[0:288]], axis=1)

    def volume_grad(x, extra=None):
        taps1[x] = dot(left1, d1[x + 1 : x + 4].reshape(3 * C1, Y * Z))
        for y in range(Y):
            piece = gather_taps(taps1.at[x], C0, Y, y, 1)
            if extra is not None:
                piece = piece + extra[y].astype(F32)
            grow[x, pl.ds(y, C0, stride=Y), :] = piece
        vgrad_out[x] = grow[x].reshape(C0, Y, Z).astype(BF16)

    for x in range(1, X - 1):
        volume_grad(x)
    b2_all.wait_recv()
    sum2 = lax.fori_loop(1, CHIPS, lambda k, t: t + rb2[k].astype(F32), pb2[chip].astype(F32))
    sc2[...] = sum2.astype(BF16)

    def c2_copy(k):
        return remote(sc2, rc2.at[k], c2_send, c2_recv, space=lax.rem(s + k, SP))

    each(1, SP, lambda k: c2_copy(k).start())
    f_wait()
    for k in range(2):
        volume_grad((X - 1) * k, fh.at[k])

    b1_all.wait_recv()
    sum1 = lax.fori_loop(1, CHIPS, lambda k, t: t + rb1[k].astype(F32), pb1[chip].astype(F32))
    sc1[...] = sum1.astype(BF16)

    def c1_copy(k):
        return remote(sc1, rc1.at[k], c1_send, c1_recv, space=lax.rem(s + k, SP))

    each(1, SP, lambda k: c1_copy(k).start())
    c2_all.wait_recv()
    full2 = lax.fori_loop(1, SP, lambda k, t: t + rc2[k].astype(F32), sc2[...].astype(F32))
    gtwo_out[...] = full2[0:R2] * (0.5 * FACTOR_TWO)

    v_drain()
    p_drain()
    e_drain()
    f_drain()
    w1_all.wait_send()
    w2_all.wait_send()
    b2_all.wait_send()
    b1_all.wait_send()
    forward1.wait_send()
    forward2.wait_send()
    pair1.wait_send()
    pair2.wait_send()
    c2_all.wait_send()
    c1_all.wait_send()

    c1_all.wait_recv()
    full1 = lax.fori_loop(1, SP, lambda k, t: t + rc1[k].astype(F32), sc1[...].astype(F32))
    gone_out[0:16, :] = full1[:, 0:C1] * FACTOR_ONE
    gone_out[16:R1, :] = pltpu.roll(full1, 64, 1)[0 : R1 - 16, 0:C1] * FACTOR_ONE


def hand_over(pooled, vgrad, gone, gtwo, pooled_to, vgrad_to, gone_to, gtwo_to, sem):
    stores = [pltpu.make_async_copy(vgrad.at[x], vgrad_to.at[0, :, x], sem.at[x]) for x in range(X)]
    stores += [
        pltpu.make_async_copy(src, dst, sem.at[X + k])
        for k, (src, dst) in enumerate(((pooled, pooled_to), (gone, gone_to), (gtwo, gtwo_to)))
    ]
    for store in stores:
        store.start()
    for store in stores:
        store.wait()


def local(volumes, w_first, w_second, cotangent):
    cot = cotangent[0, :, 0].transpose(1, 2, 0)
    hbm = pl.BlockSpec(memory_space=pltpu.HBM)
    shapes = (
        jax.ShapeDtypeStruct((2, 32, C2), BF16),
        jax.ShapeDtypeStruct((1, C0, X, Y, Z), BF16),
        jax.ShapeDtypeStruct((R1, C1), F32),
        jax.ShapeDtypeStruct((R2, C2), F32),
    )
    dma = pltpu.SemaphoreType.DMA
    vmem = pl.BlockSpec(memory_space=pltpu.VMEM)
    results = pl.pallas_call(
        kernel,
        out_shape=(
            pltpu.VMEM((2, 32, C2), BF16),
            pltpu.VMEM((X, C0, Y, Z), BF16),
            pltpu.VMEM((R1, C1), F32),
            pltpu.VMEM((R2, C2), F32),
        ),
        in_specs=[hbm] * 4,
        out_specs=(vmem,) * 4,
        scratch_shapes=[
            pltpu.VMEM((1, C0, X, Y, Z), BF16),
            pltpu.VMEM((R1, C1), BF16),
            pltpu.VMEM((R2, C2), BF16),
            pltpu.VMEM((2, 32, C2), BF16),
            pltpu.VMEM((4, C0, Y, Z), BF16),
            pltpu.VMEM((C0 * Y, Z), F32),
            pltpu.VMEM((X + 2, 9 * C0, Y * Z), BF16),
            pltpu.VMEM((X, C1, Y * Z), F32),
            pltpu.VMEM((X, C1, Y * Z), F32),
            pltpu.VMEM((2, Y // 2, C1, Z), F32),
            pltpu.VMEM((2, 2, C1, Z), BF16),
            pltpu.VMEM((2, 2, C1, Z), BF16),
            pltpu.VMEM((4, 9 * C1, Y // 2 * Z), BF16),
            pltpu.VMEM((2, C2, Y // 2 * Z), F32),
            pltpu.VMEM((2, C2, Y // 2 * Z), BF16),
            pltpu.VMEM((2, 2, C1, Z), BF16),
            pltpu.VMEM((2, 2, C1, Z), BF16),
            pltpu.VMEM((X + 4, C1, Y * Z), BF16),
            pltpu.VMEM((X, 9 * C0, Y * Z), F32),
            pltpu.VMEM((X, C0 * Y, Z), F32),
            pltpu.VMEM((18 * C1, Y // 2 * Z), F32),
            pltpu.VMEM((2, 9 * C1, Y // 2 * Z), F32),
            pltpu.VMEM((2, Y, C0, Z), BF16),
            pltpu.VMEM((2, Y, C0, Z), BF16),
            pltpu.VMEM((32, C1), F32),
            pltpu.VMEM((80, 128), BF16),
            pltpu.VMEM((CHIPS, 2, 16, 128), BF16),
            pltpu.VMEM((CHIPS, 2, 64, 128), BF16),
            pltpu.VMEM((27 * C0, C1), F32),
            pltpu.VMEM((27 * C1, C2), F32),
            pltpu.VMEM((27 * C0, C1), BF16),
            pltpu.VMEM((27 * C1, C2), BF16),
            pltpu.VMEM((C1, 27 * C0), BF16),
            pltpu.VMEM((C2, 27 * C1), BF16),
            pltpu.VMEM((27 * C0, C1), F32),
            pltpu.VMEM((27 * C1, C2), F32),
            pltpu.VMEM((CHIPS, 2, 16, 128), BF16),
            pltpu.VMEM((CHIPS, 2, 64, 128), BF16),
            pltpu.VMEM((CHIPS, 16, 128), BF16),
            pltpu.VMEM((CHIPS, 64, 128), BF16),
            pltpu.VMEM((CHIPS, 16, 128), BF16),
            pltpu.VMEM((CHIPS, 64, 128), BF16),
            pltpu.VMEM((CHIPS, 16, 128), BF16),
            pltpu.VMEM((CHIPS, 64, 128), BF16),
            pltpu.VMEM((16, 128), BF16),
            pltpu.VMEM((64, 128), BF16),
            pltpu.VMEM((SP, 16, 128), BF16),
            pltpu.VMEM((SP, 64, 128), BF16),
            dma((4,)),
            dma((4, 2)), dma((4, 2)),
            dma((4,)), dma((4,)),
            dma, dma,
            dma, dma,
            dma, dma,
            dma, dma,
            dma, dma,
            dma, dma,
        ],
        compiler_params=pltpu.CompilerParams(
            collective_id=0, has_side_effects=True, vmem_limit_bytes=VMEM_BYTES
        ),
    )(*(pltpu.with_memory_space_constraint(each, pltpu.HBM) for each in (volumes, w_first, w_second, cot)))
    pooled, vgrad, gone, gtwo = pl.pallas_call(
        hand_over,
        out_shape=shapes,
        in_specs=[vmem] * 4,
        out_specs=(hbm,) * 4,
        scratch_shapes=[dma((X + 3,))],
        compiler_params=pltpu.CompilerParams(vmem_limit_bytes=VMEM_BYTES),
    )(*results)
    return (pooled.transpose(2, 0, 1)[None, :, None], vgrad, gone, gtwo)


def solution(mesh):
    return jax.shard_map(
        local,
        mesh=mesh,
        in_specs=(
            P("dp", None, "space", None, None),
            P("dp", None),
            P("dp", None),
            P("dp", None, "space", None, None),
        ),
        out_specs=(
            P("dp", None, "space", None, None),
            P("dp", None, "space", None, None),
            P("dp", None),
            P("dp", None),
        ),
        check_vma=False,
    )
```

```python
import functools

import jax
import jax.numpy as jnp
from jax import lax
from jax.experimental import pallas as pl
from jax.experimental.pallas import tpu as pltpu
from jax.sharding import PartitionSpec as P

MESH = pl.DeviceIdType.MESH
F32 = jnp.float32
BF16 = jnp.bfloat16

DP = 32
SP = 8
CHIPS = 16
C0, C1, C2 = 32, 64, 128
X, Y, Z = 4, 8, 128
R1, R2 = 27, 54
VMEM_BYTES = 48 * 1024 * 1024
FAR_CHIPS = (12, 11, 13, 4, 10, 14, 3, 5, 9, 15, 2, 6, 8, 1, 7)
FACTOR_ONE = float(1048576) ** (-0.5)
FACTOR_TWO = float(131072) ** (-0.5)


def dot(a, b):
    return lax.dot_general(a, b, (((1,), (0,)), ((), ())), preferred_element_type=F32)


def dot_nt(a, b):
    return lax.dot_general(a, b, (((1,), (1,)), ((), ())), preferred_element_type=F32)


def lanes(rows):
    return lax.broadcasted_iota(jnp.int32, (rows, Z), 1)


def shifted(tile, by):
    moved = pltpu.roll(tile, by % Z, 1)
    at = lanes(tile.shape[0])
    keep = at >= by if by > 0 else at < Z + by
    return jnp.where(keep, moved, 0.0)


def frame_plane(source, dest, rows, count, step):
    zero = jnp.zeros((3 * rows, Z), BF16)
    dest[0 : 3 * rows, 0:Z] = zero
    dest[6 * rows : 9 * rows, (count - 1) * Z : count * Z] = zero
    for y in range(count):
        wide = source(y)
        three = [t.astype(BF16) for t in (shifted(wide, step), wide, shifted(wide, -step))]
        for b in range(3):
            to = y - b + 1
            if 0 <= to < count:
                for c in range(3):
                    row = (b * 3 + c) * rows
                    dest[row : row + rows, to * Z : (to + 1) * Z] = three[c]


def gather_taps(parts, rows, count, y, step):
    total = None
    for c in range(3):
        column = None
        for b in range(3):
            at = y - b + 1
            if 0 <= at < count:
                row = (b * 3 + c) * rows
                piece = parts[row : row + rows, at * Z : (at + 1) * Z]
                column = piece if column is None else column + piece
        if c == 0:
            column = shifted(column, -step)
        elif c == 2:
            column = shifted(column, step)
        total = column if total is None else total + column
    return total


def kernel(
    vol_in, wone_in, wtwo_in, cot_in,
    pooled_out, vgrad_out, gone_out, gtwo_out,
    vol, wone, wtwo, cot, vh, fst, s1, pre1, slope1, pp, ps, ph, s2, pre2, d2, es, eh, d1, taps1, grow, taps2, edge2, fs, fh,
    wpad, wsend, wg1, wg2, wf1, wf2, w1, w2, w1t, w2t,
    gs1, gs2, gp1, gp2, ra1, ra2, pb1, pb2, rb1, rb2, sc1, sc2, rc1, rc2,
    in_sem, halo_send, halo_recv, pair_send, pair_recv,
    w1_send, w1_recv, w2_send, w2_recv,
    b1_send, b1_recv, b2_send, b2_recv, c1_send, c1_recv, c2_send, c2_recv,
):
    d = lax.axis_index("dp")
    s = lax.axis_index("space")
    core = lax.rem(d, 2)
    chip = d // 2
    sibling = chip * 2 + 1 - core

    def remote(src, dst, ssem, rsem, **where):
        return pltpu.make_async_remote_copy(
            src_ref=src, dst_ref=dst, send_sem=ssem, recv_sem=rsem,
            device_id=where, device_id_type=MESH,
        )

    def whole(view, ssem, rsem):
        return remote(view, view, ssem, rsem, dp=sibling)

    def each(low, high, action):
        def body(k, carry):
            action(k)
            return carry

        lax.fori_loop(low, high, body, 0)

    def peer(k):
        return lax.rem(chip + k, CHIPS) * 2 + core

    def greet(**where):
        pl.semaphore_signal(barrier, inc=1, device_id=where, device_id_type=MESH)

    barrier = pltpu.get_barrier_semaphore()
    loads = [
        pltpu.make_async_copy(src, dst, in_sem.at[k])
        for k, (src, dst) in enumerate(((wone_in, wone), (wtwo_in, wtwo), (vol_in, vol), (cot_in, cot)))
    ]
    for load in loads:
        load.start()
    each(1, CHIPS, lambda k: greet(dp=peer(k)))
    each(1, SP, lambda k: greet(space=lax.rem(s + k, SP)))
    greet(dp=sibling)

    loads[0].wait()
    loads[1].wait()
    wpad[0:R1] = wone[...].astype(F32)
    wpad[R1:32] = jnp.zeros((32 - R1, C1), F32)
    wsend[0:16] = jnp.concatenate([wpad[0:16], wpad[16:32]], axis=1).astype(BF16)
    wsend[16 : 16 + R2] = wtwo[...]
    wsend[16 + R2 : 80] = jnp.zeros((64 - R2, C2), BF16)
    wg1[chip, core] = wsend[0:16]
    wg2[chip, core] = wsend[16:80]
    loads[2].wait()
    for k in range(2):
        vh[k] = vol[0, :, 0 if k == 0 else X - 1]
    pl.semaphore_wait(barrier, CHIPS - 1 + SP - 1 + 1)

    def halo(n, low_src, high_src, low_dst, high_dst):
        up = remote(high_src, low_dst, halo_send.at[n, 0], halo_recv.at[n, 0], space=lax.rem(s + 1, SP))
        down = remote(low_src, high_dst, halo_send.at[n, 1], halo_recv.at[n, 1], space=lax.rem(s + SP - 1, SP))

        def start():
            @pl.when(s < SP - 1)
            def _():
                up.start()

            @pl.when(s > 0)
            def _():
                down.start()

        def wait():
            @pl.when(s > 0)
            def _():
                up.wait_recv()

            @pl.when(s == 0)
            def _():
                low_dst[...] = jnp.zeros(low_dst.shape, BF16)

            @pl.when(s < SP - 1)
            def _():
                down.wait_recv()

            @pl.when(s == SP - 1)
            def _():
                high_dst[...] = jnp.zeros(high_dst.shape, BF16)

        def drain():
            @pl.when(s < SP - 1)
            def _():
                up.wait_send()

            @pl.when(s > 0)
            def _():
                down.wait_send()

        return start, wait, drain

    def w1_copy(k):
        return remote(wsend.at[pl.ds(0, 16)], wg1.at[chip, core], w1_send, w1_recv, dp=peer(k))

    def w2_copy(k):
        return remote(wsend.at[pl.ds(16, 64)], wg2.at[chip, core], w2_send, w2_recv, dp=peer(k))

    w1_all = whole(wg1.at[pl.ds(1, CHIPS - 1), 0], w1_send, w1_recv)
    w2_all = whole(wg2.at[pl.ds(1, CHIPS - 1), 0], w2_send, w2_recv)
    b1_all = whole(rb1.at[pl.ds(1, CHIPS - 1)], b1_send, b1_recv)
    b2_all = whole(rb2.at[pl.ds(1, CHIPS - 1)], b2_send, b2_recv)
    c1_all = whole(rc1.at[pl.ds(1, SP - 1)], c1_send, c1_recv)
    c2_all = whole(rc2.at[pl.ds(1, SP - 1)], c2_send, c2_recv)
    for k in FAR_CHIPS:
        w1_copy(k).start()
    v_start, v_wait, v_drain = halo(0, vh.at[0], vh.at[1], vh.at[2], vh.at[3])
    v_start()
    for k in FAR_CHIPS:
        w2_copy(k).start()

    def frame_input(plane, dest):
        fst[...] = plane.astype(F32).reshape(C0 * Y, Z)
        frame_plane(lambda y: fst[pl.ds(y, C0, stride=Y), :], dest, C0, Y, 1)

    each(0, X, lambda k: frame_input(vol[0, :, k], s1.at[k + 1]))

    w1_all.wait_recv()
    forward1 = remote(wg1.at[:, core], wg1.at[:, core], pair_send.at[0], pair_recv.at[0], dp=sibling)
    forward1.start()
    v_wait()
    each(0, 2, lambda k: frame_input(vh[k + 2], s1.at[k * (X + 1)]))
    forward1.wait_recv()
    for k in range(DP):
        block = wg1[k // 2, k % 2].astype(F32)
        wf1[R1 * k : R1 * k + 16, 0:C1] = block[:, 0:C1]
        wf1[R1 * k + 16 : R1 * k + R1, 0:C1] = pltpu.roll(block, 64, 1)[0 : R1 - 16, 0:C1]
    w1[...] = wf1[...].astype(BF16)
    w1t[...] = wf1[...].T.astype(BF16)

    even = lax.rem(lanes(C1), 2) == 0

    for x in range(X):
        pre1[x] = dot(w1t[...], s1[x : x + 3].reshape(27 * C0, Y * Z))
    for h in range(2):
        for y in range(Y // 2):
            total = jnp.zeros((C1, Z), F32)
            for k in range(2):
                for j in range(2):
                    at = slice((2 * y + j) * Z, (2 * y + j + 1) * Z)
                    t = pre1[2 * h + k, :, at]
                    sigma = jax.nn.sigmoid(t)
                    total = total + t * sigma
                    slope1[2 * h + k, :, at] = sigma * (1.0 + t * (1.0 - sigma)) * 0.125
            other = jnp.where(even, pltpu.roll(total, Z - 1, 1), pltpu.roll(total, 1, 1))
            pp[h, y] = (total + other) * 0.125

    for h in range(2):
        for y in range(2):
            ps[h, y] = jnp.where(even, pp[h, 2 * y], pp[h, 2 * y + 1]).astype(BF16)
    p_start, p_wait, p_drain = halo(1, ps.at[0], ps.at[1], ph.at[0], ph.at[1])
    p_start()

    def apart(pairs, y):
        wide = pairs[y // 2].astype(F32)
        if y % 2 == 0:
            return jnp.where(even, wide, pltpu.roll(wide, 1, 1))
        return jnp.where(even, pltpu.roll(wide, Z - 1, 1), wide)

    w2_all.wait_recv()
    forward2 = remote(wg2.at[:, core], wg2.at[:, core], pair_send.at[1], pair_recv.at[1], dp=sibling)
    forward2.start()
    for h in range(2):
        frame_plane(lambda y: pp[h, y], s2.at[h + 1], C1, Y // 2, 2)
    forward2.wait_recv()
    for k in range(DP):
        wf2[R2 * k : R2 * k + R2, :] = wg2[k // 2, k % 2].astype(F32)[0:R2]
    w2[...] = wf2[...].astype(BF16)
    w2t[...] = wf2[...].T.astype(BF16)
    p_wait()
    for h in range(2):
        frame_plane(lambda y: apart(ph[h], y), s2.at[3 * h], C1, Y // 2, 2)

    loads[3].wait()
    spread = jnp.where(
        lax.broadcasted_iota(jnp.int32, (32, Z), 1) // 4 == lax.broadcasted_iota(jnp.int32, (32, Z), 0), 1.0, 0.0
    ).astype(BF16)
    squeeze = jnp.where(
        lax.broadcasted_iota(jnp.int32, (32, Z), 1) // 4 == lax.broadcasted_iota(jnp.int32, (32, Z), 0), 0.5, 0.0
    ).astype(BF16)
    for x in range(2):
        pre2[x] = dot(w2t[...], s2[x : x + 3].reshape(27 * C1, Y // 2 * Z))
    sums = []
    for y in range(2):
        spreaded = lax.dot_general(cot[y], spread, (((0,), (0,)), ((), ())), preferred_element_type=F32) * 0.125
        total = jnp.zeros((C2, Z), F32)
        for x in range(2):
            for j in range(2):
                at = slice((2 * y + j) * Z, (2 * y + j + 1) * Z)
                t = pre2[x, :, at]
                sigma = jax.nn.sigmoid(t)
                total = total + t * sigma
                d2[x, :, at] = (spreaded * (sigma * (1.0 + t * (1.0 - sigma)))).astype(BF16)
        sums.append(total)

    for k in range(2):
        edge2[k] = dot(w2[1152 * k : 1152 * k + 576], d2[k])
        for y in range(2):
            a, b = (gather_taps(edge2.at[k], C1, Y // 2, 2 * y + j, 2) for j in range(2))
            es[k, y] = jnp.where(even, a, b).astype(BF16)
    e_start, e_wait, e_drain = halo(2, es.at[0], es.at[1], eh.at[0], eh.at[1])
    e_start()

    parts = [dot_nt(s2[k], d2[...].reshape(2 * C2, Y // 2 * Z)) for k in range(4)]
    for a in range(3):
        gs2[a * 576 : (a + 1) * 576, :] = parts[a][:, 0:128] + parts[a + 1][:, 128:256]
    for k in range(DP):
        gp2[k // 2, k % 2, 0:R2, :] = gs2[R2 * k : R2 * k + R2, :].astype(BF16)
        gp2[k // 2, k % 2, R2:64, :] = jnp.zeros((64 - R2, C2), BF16)
    pair2 = remote(gp2.at[:, 1 - core], ra2, pair_send.at[2], pair_recv.at[2], dp=sibling)
    pair2.start()

    for x in range(2):
        left = jnp.concatenate([w2[(x + 1) * 576 : (x + 2) * 576], w2[x * 576 : (x + 1) * 576]], axis=1)
        taps2[x * 576 : (x + 1) * 576] = dot(left, d2[...].reshape(2 * C2, Y // 2 * Z))

    for y in range(2):
        total = sums[y] * 0.125
        high = total.astype(BF16)
        low = (total - high.astype(F32)).astype(BF16)
        pooled_out[y] = (dot_nt(squeeze, high) + dot_nt(squeeze, low)).astype(BF16)

    pair2.wait_recv()

    def add_pair2(k):
        pb2[k] = (gp2[k, core].astype(F32) + ra2[k].astype(F32)).astype(BF16)

    each(0, CHIPS, add_pair2)

    def b2_copy(k):
        return remote(
            pb2.at[lax.rem(chip + k, CHIPS)], rb2.at[k], b2_send, b2_recv, dp=peer(k)
        )

    for k in FAR_CHIPS:
        b2_copy(k).start()

    e_wait()
    for k in range(2):
        d1[1 + (X + 1) * k] = jnp.zeros((C1, Y * Z), BF16)
    for x in range(2):
        for y in range(Y // 2):
            grad = gather_taps(taps2.at[x * 576 : (x + 1) * 576], C1, Y // 2, y, 2) + apart(eh[x], y)
            grad = grad.astype(BF16).astype(F32)
            for k in range(2):
                for j in range(2):
                    at = slice((2 * y + j) * Z, (2 * y + j + 1) * Z)
                    d1[2 * x + k + 2, :, at] = (grad * slope1[2 * x + k, :, at]).astype(BF16)

    parts = [dot_nt(s1[k], d1[2 : X + 2].reshape(X * C1, Y * Z)) for k in range(X + 2)]
    for a in range(3):
        low = parts[a][:, 0:128] + parts[a + 2][:, 128:256]
        high = parts[a + 1][:, 0:128] + parts[a + 3][:, 128:256]
        gs1[a * 288 : (a + 1) * 288, :] = (low + pltpu.roll(high, 64, 1))[:, 0:C1]
    for k in range(DP):
        head = gs1[R1 * k : R1 * k + 16, :].astype(BF16)
        tail = jnp.concatenate(
            [gs1[R1 * k + 16 : R1 * k + R1, :], jnp.zeros((32 - R1, C1), F32)], axis=0
        ).astype(BF16)
        gp1[k // 2, k % 2] = jnp.concatenate([head, tail], axis=1)
    pair1 = remote(gp1.at[:, 1 - core], ra1, pair_send.at[3], pair_recv.at[3], dp=sibling)
    pair1.start()

    for k in range(2):
        taps1[k] = dot(w1[576 * k : 576 * k + 288], d1[2 + (X - 1) * k])
        for y in range(Y):
            fs[k, y] = gather_taps(taps1.at[k], C0, Y, y, 1).astype(BF16)
    f_start, f_wait, f_drain = halo(3, fs.at[0], fs.at[1], fh.at[0], fh.at[1])
    f_start()

    pair1.wait_recv()

    def add_pair1(k):
        pb1[k] = (gp1[k, core].astype(F32) + ra1[k].astype(F32)).astype(BF16)

    each(0, CHIPS, add_pair1)

    def b1_copy(k):
        return remote(
            pb1.at[lax.rem(chip + k, CHIPS)], rb1.at[k], b1_send, b1_recv, dp=peer(k)
        )

    for k in FAR_CHIPS:
        b1_copy(k).start()

    left1 = jnp.concatenate([w1[576:864], w1[288:576], w1[0:288]], axis=1)

    def volume_grad(x, extra=None):
        taps1[x] = dot(left1, d1[x + 1 : x + 4].reshape(3 * C1, Y * Z))
        for y in range(Y):
            piece = gather_taps(taps1.at[x], C0, Y, y, 1)
            if extra is not None:
                piece = piece + extra[y].astype(F32)
            grow[x, pl.ds(y, C0, stride=Y), :] = piece
        vgrad_out[x] = grow[x].reshape(C0, Y, Z).astype(BF16)

    for x in range(1, X - 1):
        volume_grad(x)
    b2_all.wait_recv()
    sum2 = lax.fori_loop(1, CHIPS, lambda k, t: t + rb2[k].astype(F32), pb2[chip].astype(F32))
    sc2[...] = sum2.astype(BF16)

    def c2_copy(k):
        return remote(sc2, rc2.at[k], c2_send, c2_recv, space=lax.rem(s + k, SP))

    each(1, SP, lambda k: c2_copy(k).start())
    f_wait()
    for k in range(2):
        volume_grad((X - 1) * k, fh.at[k])

    b1_all.wait_recv()
    sum1 = lax.fori_loop(1, CHIPS, lambda k, t: t + rb1[k].astype(F32), pb1[chip].astype(F32))
    sc1[...] = sum1.astype(BF16)

    def c1_copy(k):
        return remote(sc1, rc1.at[k], c1_send, c1_recv, space=lax.rem(s + k, SP))

    each(1, SP, lambda k: c1_copy(k).start())
    c2_all.wait_recv()
    full2 = lax.fori_loop(1, SP, lambda k, t: t + rc2[k].astype(F32), sc2[...].astype(F32))
    gtwo_out[...] = full2[0:R2] * (0.5 * FACTOR_TWO)

    v_drain()
    p_drain()
    e_drain()
    f_drain()
    w1_all.wait_send()
    w2_all.wait_send()
    b2_all.wait_send()
    b1_all.wait_send()
    forward1.wait_send()
    forward2.wait_send()
    pair1.wait_send()
    pair2.wait_send()
    c2_all.wait_send()
    c1_all.wait_send()

    c1_all.wait_recv()
    full1 = lax.fori_loop(1, SP, lambda k, t: t + rc1[k].astype(F32), sc1[...].astype(F32))
    gone_out[0:16, :] = full1[:, 0:C1] * FACTOR_ONE
    gone_out[16:R1, :] = pltpu.roll(full1, 64, 1)[0 : R1 - 16, 0:C1] * FACTOR_ONE


def hand_over(pooled, vgrad, gone, gtwo, pooled_to, vgrad_to, gone_to, gtwo_to, sem):
    stores = [pltpu.make_async_copy(vgrad.at[x], vgrad_to.at[0, :, x], sem.at[x]) for x in range(X)]
    stores += [
        pltpu.make_async_copy(src, dst, sem.at[X + k])
        for k, (src, dst) in enumerate(((pooled, pooled_to), (gone, gone_to), (gtwo, gtwo_to)))
    ]
    for store in stores:
        store.start()
    for store in stores:
        store.wait()


def local(volumes, w_first, w_second, cotangent):
    cot = cotangent[0, :, 0].transpose(1, 2, 0)
    hbm = pl.BlockSpec(memory_space=pltpu.HBM)
    shapes = (
        jax.ShapeDtypeStruct((2, 32, C2), BF16),
        jax.ShapeDtypeStruct((1, C0, X, Y, Z), BF16),
        jax.ShapeDtypeStruct((R1, C1), F32),
        jax.ShapeDtypeStruct((R2, C2), F32),
    )
    dma = pltpu.SemaphoreType.DMA
    vmem = pl.BlockSpec(memory_space=pltpu.VMEM)
    results = pl.pallas_call(
        kernel,
        out_shape=(
            pltpu.VMEM((2, 32, C2), BF16),
            pltpu.VMEM((X, C0, Y, Z), BF16),
            pltpu.VMEM((R1, C1), F32),
            pltpu.VMEM((R2, C2), F32),
        ),
        in_specs=[hbm] * 4,
        out_specs=(vmem,) * 4,
        scratch_shapes=[
            pltpu.VMEM((1, C0, X, Y, Z), BF16),
            pltpu.VMEM((R1, C1), BF16),
            pltpu.VMEM((R2, C2), BF16),
            pltpu.VMEM((2, 32, C2), BF16),
            pltpu.VMEM((4, C0, Y, Z), BF16),
            pltpu.VMEM((C0 * Y, Z), F32),
            pltpu.VMEM((X + 2, 9 * C0, Y * Z), BF16),
            pltpu.VMEM((X, C1, Y * Z), F32),
            pltpu.VMEM((X, C1, Y * Z), F32),
            pltpu.VMEM((2, Y // 2, C1, Z), F32),
            pltpu.VMEM((2, 2, C1, Z), BF16),
            pltpu.VMEM((2, 2, C1, Z), BF16),
            pltpu.VMEM((4, 9 * C1, Y // 2 * Z), BF16),
            pltpu.VMEM((2, C2, Y // 2 * Z), F32),
            pltpu.VMEM((2, C2, Y // 2 * Z), BF16),
            pltpu.VMEM((2, 2, C1, Z), BF16),
            pltpu.VMEM((2, 2, C1, Z), BF16),
            pltpu.VMEM((X + 4, C1, Y * Z), BF16),
            pltpu.VMEM((X, 9 * C0, Y * Z), F32),
            pltpu.VMEM((X, C0 * Y, Z), F32),
            pltpu.VMEM((18 * C1, Y // 2 * Z), F32),
            pltpu.VMEM((2, 9 * C1, Y // 2 * Z), F32),
            pltpu.VMEM((2, Y, C0, Z), BF16),
            pltpu.VMEM((2, Y, C0, Z), BF16),
            pltpu.VMEM((32, C1), F32),
            pltpu.VMEM((80, 128), BF16),
            pltpu.VMEM((CHIPS, 2, 16, 128), BF16),
            pltpu.VMEM((CHIPS, 2, 64, 128), BF16),
            pltpu.VMEM((27 * C0, C1), F32),
            pltpu.VMEM((27 * C1, C2), F32),
            pltpu.VMEM((27 * C0, C1), BF16),
            pltpu.VMEM((27 * C1, C2), BF16),
            pltpu.VMEM((C1, 27 * C0), BF16),
            pltpu.VMEM((C2, 27 * C1), BF16),
            pltpu.VMEM((27 * C0, C1), F32),
            pltpu.VMEM((27 * C1, C2), F32),
            pltpu.VMEM((CHIPS, 2, 16, 128), BF16),
            pltpu.VMEM((CHIPS, 2, 64, 128), BF16),
            pltpu.VMEM((CHIPS, 16, 128), BF16),
            pltpu.VMEM((CHIPS, 64, 128), BF16),
            pltpu.VMEM((CHIPS, 16, 128), BF16),
            pltpu.VMEM((CHIPS, 64, 128), BF16),
            pltpu.VMEM((CHIPS, 16, 128), BF16),
            pltpu.VMEM((CHIPS, 64, 128), BF16),
            pltpu.VMEM((16, 128), BF16),
            pltpu.VMEM((64, 128), BF16),
            pltpu.VMEM((SP, 16, 128), BF16),
            pltpu.VMEM((SP, 64, 128), BF16),
            dma((4,)),
            dma((4, 2)), dma((4, 2)),
            dma((4,)), dma((4,)),
            dma, dma,
            dma, dma,
            dma, dma,
            dma, dma,
            dma, dma,
            dma, dma,
        ],
        compiler_params=pltpu.CompilerParams(
            collective_id=0, has_side_effects=True, vmem_limit_bytes=VMEM_BYTES
        ),
    )(*(pltpu.with_memory_space_constraint(each, pltpu.HBM) for each in (volumes, w_first, w_second, cot)))
    pooled, vgrad, gone, gtwo = pl.pallas_call(
        hand_over,
        out_shape=shapes,
        in_specs=[vmem] * 4,
        out_specs=(hbm,) * 4,
        scratch_shapes=[dma((X + 3,))],
        compiler_params=pltpu.CompilerParams(vmem_limit_bytes=VMEM_BYTES),
    )(*results)
    return (pooled.transpose(2, 0, 1)[None, :, None], vgrad, gone, gtwo)


def solution(mesh):
    return jax.shard_map(
        local,
        mesh=mesh,
        in_specs=(
            P("dp", None, "space", None, None),
            P("dp", None),
            P("dp", None),
            P("dp", None, "space", None, None),
        ),
        out_specs=(
            P("dp", None, "space", None, None),
            P("dp", None, "space", None, None),
            P("dp", None),
            P("dp", None),
        ),
        check_vma=False,
    )
```
